32 devices in a mesh: tm: 8 (over z, core), space: 4 (over y, x).
Axes of the slice: x: 2, y: 2, z: 4, core: 2. Of those that a mesh axis runs over, the one named last changes fastest.
Arguments:
- start_states: float32 [8, 2, 12, 192, 256], P('tm', None, None, 'space'), may hold values from -6 to 6
- wet_levels: int32 [192, 256], P('space'), may hold values from 0 to 12
- advection: float32 [192, 256], P('space'), may hold values from 0.05 to 0.3
- forcing: float32 [192, 256], P('space'), may hold values from -6 to 6
- rates: float32 [4, 12], replicated, may hold values from 0.02 to 0.12
Outputs:
- new_states: float32 [8, 2, 12, 192, 256], P('tm', None, None, 'space')
The draws below stay inside these ranges and needn't reach their ends.
All inputs are finite; a program needn't handle non-finite values.
Results may differ from the reference program's by a relative error of at most 0.00002.
Values sent between devices are 32-bit elements; how exact they have to be, the bound alone decides.
A program may use at most 128 MiB of HBM per device.

```python
import math
import jax
import jax.numpy as jnp
from jax import lax

TR = 2
LEV = 12
LAT = 256
STEPS = 4
SECTIONS = 4
COARSEN = 4
SEG = 8
NLON = 192
N_TM = 8


def plant(result, stream_key, smallest, top_value):
    spot = [jax.random.randint(jax.random.fold_in(stream_key, axis), (), 0, length) for axis, length in enumerate(result.shape)]
    main_axis = result.shape.index(max(result.shape))
    neighbour = spot[:main_axis] + [(spot[main_axis] + 1) % result.shape[main_axis]] + spot[main_axis + 1:]
    return result.at[tuple(spot)].set(smallest).at[tuple(neighbour)].set(top_value)


def block_scale(own_key, extent, cuts, least, top_value):
    gain, own = 1.0, jax.random.fold_in(own_key, 6)
    for dim, shards_of in cuts:
        steps = jnp.exp(jax.random.uniform(jax.random.fold_in(own, dim), (shards_of,), jnp.float32, least / len(cuts), top_value / len(cuts)))
        gain = gain * jnp.repeat(steps, extent[dim] // shards_of).reshape([-1 if axis == dim else 1 for axis in range(len(extent))])
    return gain


def normal_values(key, shape, scale, reach, cuts=(), kind=jnp.bfloat16):
    entries = scale * jax.random.normal(key, shape, jnp.float32)
    if cuts:
        entries = entries * block_scale(key, shape, cuts, -0.22, 0.18)
    return jnp.clip(entries, -reach, reach).astype(kind)


def setup_inputs(seed: int = 0) -> dict:
    splits = jax.random.split(jax.random.key(seed), 6)
    return {
        "start_states": normal_values(splits[0], (SEG, TR, LEV, NLON, LAT), 1.0, 6.0, ((0, 8), (3, 4)), jnp.float32),
        "wet_levels": plant(jax.random.randint(splits[1], (NLON, LAT), 0, LEV + 1), jax.random.fold_in(splits[1], 1), 0, LEV).astype(jnp.int32),
        "advection": jnp.clip(0.05 + 0.25 * jax.random.uniform(splits[2], (NLON, LAT), jnp.float32) ** block_scale(splits[2], (NLON, LAT), ((0, 4),), -0.2, 0.2), 0.05, 0.3),
        "forcing": normal_values(splits[3], (NLON, LAT), 1.0, 6.0, ((0, 4),), jnp.float32),
        "rates": jnp.clip(jnp.exp(jax.random.uniform(splits[4], (4, LEV), jnp.float32, math.log(0.02), math.log(0.12))), 0.02, 0.12),
    }


def pad_lon(field, width):
    return jnp.concatenate([field[..., -width:, :], field, field[..., :width, :]], axis=-2)


def restrict(field):
    shape = field.shape[:-2] + (field.shape[-2] // COARSEN, COARSEN, field.shape[-1] // COARSEN, COARSEN)
    return jnp.mean(field.reshape(shape), axis=(-3, -1))


def prolong(field):
    return jnp.repeat(jnp.repeat(field, COARSEN, axis=-2), COARSEN, axis=-1)


def season_at(position, year):
    return 1.0 + 0.6 * jnp.sin(2.0 * math.pi * position / year)


def advance(padded, mask_pad, flow_rate, forcing, coeffs, relax, season):
    kappa, vertical, growth, remin = coeffs[0], coeffs[1], coeffs[2], coeffs[3]
    centre = padded[:, :, 1:-1, :]
    mask = mask_pad[:, 1:-1, :]
    east = padded[:, :, 2:, :]
    west = padded[:, :, :-2, :]
    mask_east = mask_pad[:, 2:, :]
    mask_west = mask_pad[:, :-2, :]
    zero_row = jnp.zeros(centre.shape[:-1] + (1,), jnp.float32)
    north = jnp.concatenate([centre[..., 1:], zero_row], axis=-1)
    south = jnp.concatenate([zero_row, centre[..., :-1]], axis=-1)
    zero_mrow = jnp.zeros(mask.shape[:-1] + (1,), jnp.float32)
    mask_north = jnp.concatenate([mask[..., 1:], zero_mrow], axis=-1)
    mask_south = jnp.concatenate([zero_mrow, mask[..., :-1]], axis=-1)
    spread = (mask_east * (east - centre) + mask_west * (west - centre)
              + mask_north * (north - centre) + mask_south * (south - centre))
    carried = flow_rate * mask_west * (west - centre)
    zero_level = jnp.zeros((centre.shape[0], 1) + centre.shape[2:], jnp.float32)
    deeper = jnp.concatenate([centre[:, 1:], zero_level], axis=1)
    shallower = jnp.concatenate([zero_level, centre[:, :-1]], axis=1)
    zero_layer = jnp.zeros((1,) + mask.shape[1:], jnp.float32)
    mask_deeper = jnp.concatenate([mask[1:], zero_layer], axis=0)
    mask_shallower = jnp.concatenate([zero_layer, mask[:-1]], axis=0)
    upper_rate = jnp.concatenate([jnp.zeros((1,), jnp.float32), vertical[:-1]])
    column = (vertical[:, None, None] * mask_deeper * (deeper - centre)
              + upper_rate[:, None, None] * mask_shallower * (shallower - centre))
    mixed = centre + kappa[:, None, None] * spread + carried + column
    produced = growth[:, None, None] * season * mixed[0]
    respired = remin[:, None, None] * mixed[1]
    nutrient = mixed[0] - produced + respired
    nutrient = nutrient.at[0].add(relax * (forcing - mixed[0, 0]))
    organic = mixed[1] + produced - respired
    return mask * jnp.stack([nutrient, organic])


def reference(start_states, wet_levels, advection, forcing, rates):
    levels = jnp.arange(LEV).astype(jnp.int32)
    mask = (levels[:, None, None] < wet_levels[None]).astype(jnp.float32)
    mask_pad = pad_lon(mask, 1)
    coarse_mask_pad = pad_lon(restrict(mask), 1)
    coarse_flow = restrict(advection) * (STEPS / COARSEN)
    coarse_forcing = restrict(forcing)
    scale = jnp.array([STEPS / COARSEN ** 2, STEPS, STEPS, STEPS], jnp.float32)
    coarse_rates = rates * scale[:, None]
    year = STEPS * N_TM
    segments = jnp.arange(N_TM).astype(jnp.float32)

    def fine_segment(inputs):
        state, seg = inputs
        for step in range(STEPS):
            state = advance(pad_lon(state, 1), mask_pad, advection, forcing, rates, 0.2,
                            season_at(seg * STEPS + step + 0.5, year))
        return state

    def coarse_one(coarse, seg):
        return advance(pad_lon(coarse, 1), coarse_mask_pad, coarse_flow, coarse_forcing, coarse_rates,
                       0.2 * STEPS, season_at(seg * STEPS + STEPS * 0.5, year))

    def coarse_all(coarse):
        return jax.vmap(coarse_one)(coarse, segments)

    fine_end = lax.map(fine_segment, (start_states, segments))
    restricted = restrict(start_states)
    jump = fine_end - prolong(coarse_all(restricted))
    jump_coarse = restrict(jump)
    coarse = restricted
    for section in range(SECTIONS):
        coarse = jnp.roll(coarse_all(coarse) + jump_coarse, 1, axis=0)
    return jnp.roll(prolong(coarse_all(coarse)) + jump, 1, axis=0)
```

```python
import math

import jax
import jax.numpy as jnp
from jax import lax
from jax.experimental import pallas as pl
from jax.experimental.pallas import tpu as pltpu
from jax.sharding import PartitionSpec as P

STEPS = 4
SECTIONS = 4
COARSEN = 4
RELAX = 0.2
HALO = 8
WIDE = COARSEN * SECTIONS
HIGH = lax.Precision.HIGHEST
MESH = pl.DeviceIdType.MESH


def season_at(position, year):
    return 1.0 + 0.6 * jnp.sin(2.0 * math.pi * position / year)


def iota(shape, dim):
    return lax.broadcasted_iota(jnp.int32, shape, dim)


def dot(a, b):
    return jnp.dot(a, b, precision=HIGH, preferred_element_type=jnp.float32)


def kernel(
    start_ref, wet_ref, flow_ref, forcing_ref, rates_ref, season_ref, out_ref,
    s_ref, a_ref, b_ref, end_ref, got_ref, diag_ref, aux_ref,
    coef_ref, first_ref, jump_ref, x_ref, xl_ref, xr_ref, jl_ref, jr_ref,
    o_ref, ol_ref, or_ref, pl_ref, pr_ref,
    local_sem, send_sem, recv_sem,
):
    tracers, levels, nf, lat = end_ref.shape
    nc = nf // COARSEN
    lc = lat // COARSEN
    lanes = 2 * lc
    window = coef_ref.shape[2]
    rows = nf + 2 * HALO
    tm, n_tm = lax.axis_index("tm"), lax.axis_size("tm")
    space, n_space = lax.axis_index("space"), lax.axis_size("space")
    after, before = lax.rem(tm + 1, n_tm), lax.rem(tm + n_tm - 1, n_tm)
    right, left = lax.rem(space + 1, n_space), lax.rem(space + n_space - 1, n_space)

    barrier = pltpu.get_barrier_semaphore()
    for i, j in ((tm, left), (tm, right), (before, space), (before, left), (before, right)):
        pl.semaphore_signal(barrier, inc=1, device_id=(i, j), device_id_type=MESH)

    load = pltpu.make_async_copy(
        start_ref.at[0], s_ref.at[:, pl.ds(1, levels), pl.ds(HALO, nf), :], local_sem
    )
    load.start()
    mid = pl.ds(WIDE, nf)
    aux_ref[0, mid, :] = wet_ref[...].astype(jnp.float32)
    aux_ref[1, mid, :] = flow_ref[...]
    aux_ref[2, mid, :] = forcing_ref[...]
    pl.semaphore_wait(barrier, 5)

    def send(index, src, dst, i, j):
        copy = pltpu.make_async_remote_copy(
            src_ref=src, dst_ref=dst, send_sem=send_sem.at[index], recv_sem=recv_sem.at[index],
            device_id=(i, j), device_id_type=MESH,
        )
        copy.start()
        return copy

    sends = [
        send(0, aux_ref.at[:, pl.ds(nf, WIDE), :], aux_ref.at[:, pl.ds(0, WIDE), :], tm, right),
        send(1, aux_ref.at[:, pl.ds(WIDE, WIDE), :],
             aux_ref.at[:, pl.ds(WIDE + nf, WIDE), :], tm, left),
        send(2, start_ref.at[0, :, :, pl.ds(nf - HALO, HALO), :],
             s_ref.at[:, pl.ds(1, levels), pl.ds(0, HALO), :], tm, right),
        send(3, start_ref.at[0, :, :, pl.ds(0, HALO), :],
             s_ref.at[:, pl.ds(1, levels), pl.ds(HALO + nf, HALO), :], tm, left),
    ]

    zero = jnp.zeros((tracers, rows, lat), jnp.float32)
    for ref in (s_ref, a_ref, b_ref):
        ref[:, 0] = zero
        ref[:, levels + 1] = zero

    sends[0].wait_recv()
    sends[1].wait_recv()
    fine = pl.ds(WIDE - HALO, rows)
    wide = aux_ref[0, fine, :]
    lane = iota((rows, lat), 1)
    wet_e = pltpu.roll(wide, rows - 1, 0)
    wet_w = pltpu.roll(wide, 1, 0)
    wet_n = jnp.where(lane == lat - 1, 0.0, pltpu.roll(wide, lat - 1, 1))
    wet_s = jnp.where(lane == 0, 0.0, pltpu.roll(wide, 1, 1))
    flow = aux_ref[1, fine, :]
    for l in range(levels):
        k = rates_ref[0, l]
        west = jnp.where(wet_w > l, 1.0, 0.0)
        count = west
        for other in (wet_e, wet_n, wet_s):
            count = count + jnp.where(other > l, 1.0, 0.0)
        total = 1.0 - k * count - flow * west
        if l:
            total = total - rates_ref[1, l - 1]
        if l < levels - 1:
            total = total - jnp.where(wide > l + 1, rates_ref[1, l], 0.0)
        diag_ref[l] = total
    load.wait()
    sends[2].wait_recv()
    sends[3].wait_recv()

    def fine_step(src, dst, step):
        season = season_ref[step]

        def level(l, carry):
            k, v, g, r = (rates_ref[i, l] for i in range(4))
            upper = rates_ref[1, lax.rem(l + levels - 1, levels)]
            lf = l.astype(jnp.float32)
            wet = aux_ref[0, fine, :]
            here = wet > lf
            speed = aux_ref[1, fine, :] + k
            centre = diag_ref[l]
            lane = iota((rows, lat), 1)
            mixed = []
            for t in range(tracers):
                u = src[t, l + 1]
                up = src[t, l]
                down = src[t, l + 2]
                if step == 0:
                    u = jnp.where(here, u, 0.0)
                    up = jnp.where(wet > lf - 1.0, up, 0.0)
                    down = jnp.where(wet > lf + 1.0, down, 0.0)
                east = pltpu.roll(u, rows - 1, 0)
                west = pltpu.roll(u, 1, 0)
                north = jnp.where(lane == lat - 1, 0.0, pltpu.roll(u, lat - 1, 1))
                south = jnp.where(lane == 0, 0.0, pltpu.roll(u, 1, 1))
                mixed.append(
                    centre * u + k * (east + north + south) + speed * west + v * down + upper * up
                )
            grown = g * season
            q = jnp.where(l == 0, RELAX, 0.0)
            nutrient = mixed[0] * (1.0 - grown - q) + r * mixed[1] + q * aux_ref[2, fine, :]
            organic = mixed[1] * (1.0 - r) + grown * mixed[0]
            nutrient = jnp.where(here, nutrient, 0.0)
            organic = jnp.where(here, organic, 0.0)
            if step < STEPS - 1:
                dst[0, l + 1] = nutrient
                dst[1, l + 1] = organic
            else:
                dst[0, l] = nutrient[HALO:HALO + nf]
                dst[1, l] = organic[HALO:HALO + nf]
            return carry

        lax.fori_loop(0, levels, level, 0)

    fine_step(s_ref, a_ref, 0)
    fine_step(a_ref, b_ref, 1)
    fine_step(b_ref, a_ref, 2)
    fine_step(a_ref, end_ref, 3)

    quarter = 1.0 / COARSEN
    fold0 = jnp.where(iota((lat, lanes), 0) // COARSEN == iota((lat, lanes), 1), quarter, 0.0)
    fold1 = jnp.where(iota((lat, lanes), 0) // COARSEN + lc == iota((lat, lanes), 1), quarter, 0.0)
    both = fold0 + fold1

    def gather_rows(count, base):
        shape = (window, count)
        same = iota(shape, 1) // COARSEN + base == iota(shape, 0)
        return jnp.where(same, quarter, 0.0)

    row = iota((window, lanes), 0)
    col = iota((window, lanes), 1)
    inner = (row >= SECTIONS) & (row < SECTIONS + nc)
    to_right = iota((8, lanes), 0) < SECTIONS
    tail = iota((8, lanes), 0) + (window - 8)
    to_left = (tail >= SECTIONS + nc) & (tail < 2 * SECTIONS + nc)

    def halo_parts(value):
        low = jnp.where(to_right, pltpu.roll(value, window - nc, 0)[:8], 0.0)
        high = jnp.where(to_left, pltpu.roll(value, nc, 0)[window - 8:], 0.0)
        return low, high

    centre_rows = gather_rows(nf, SECTIONS)
    for l in range(levels):
        part = dot(centre_rows, dot(end_ref[0, l], fold0) + dot(end_ref[1, l], fold1))
        o_ref[0, l] = part
        low, high = halo_parts(part)
        ol_ref[l] = low
        or_ref[l] = high
    sends += [
        send(4, o_ref.at[0], x_ref.at[0], after, space),
        send(5, ol_ref, xl_ref, after, right),
        send(6, or_ref, xr_ref, after, left),
    ]
    chunk = levels // SECTIONS
    big = []

    def send_chunk(index):
        part = pl.ds(index * chunk, chunk)
        big.append(send(13 + index, end_ref.at[:, part], got_ref.at[:, part], after, space))

    send_chunk(0)

    wide_rows = gather_rows(nf + 2 * WIDE, 0)
    c_flow = dot(wide_rows, dot(aux_ref[1], both)) * (STEPS / COARSEN)
    c_forcing = dot(wide_rows, dot(aux_ref[2], both))
    wet = aux_ref[0]
    masks = []
    for l in range(levels):
        mask = jnp.where(wet > l, 1.0, 0.0)
        masks.append(
            jnp.dot(wide_rows, jnp.dot(mask, both, preferred_element_type=jnp.float32),
                    preferred_element_type=jnp.float32)
        )
    season = season_ref[STEPS]
    is_nutrient = col < lc
    edge_n = (col == lc - 1) | (col == lanes - 1)
    edge_s = (col == 0) | (col == lc)
    for l in range(levels):
        m = masks[l]
        k = rates_ref[0, l] * (STEPS / COARSEN**2)
        g = rates_ref[2, l] * STEPS * season
        r = rates_ref[3, l] * STEPS
        q = RELAX * STEPS if l == 0 else 0.0
        m_w = pltpu.roll(m, 1, 0)
        east = k * pltpu.roll(m, window - 1, 0)
        west = (k + c_flow) * m_w
        north = k * jnp.where(edge_n, 0.0, pltpu.roll(m, lanes - 1, 1))
        south = k * jnp.where(edge_s, 0.0, pltpu.roll(m, 1, 1))
        total = 1.0 - east - west - north - south
        if l < levels - 1:
            down = rates_ref[1, l] * STEPS * masks[l + 1]
            total = total - down
            coef_ref[4, l] = down
        if l:
            up = rates_ref[1, l - 1] * STEPS * masks[l - 1]
            total = total - up
            coef_ref[5, l] = up
        coef_ref[0, l] = east
        coef_ref[1, l] = west
        coef_ref[2, l] = north
        coef_ref[3, l] = south
        coef_ref[6, l] = total
        coef_ref[7, l] = m * jnp.where(is_nutrient, 1.0 - g - q, 1.0 - r)
        coef_ref[8, l] = m * jnp.where(is_nutrient, r, g)
    surface = masks[0] * jnp.where(is_nutrient, RELAX * STEPS * c_forcing, 0.0)

    def coarse_step(load_level):
        fields = [load_level(l) for l in range(levels)]
        results = []
        for l in range(levels):
            u = fields[l]
            w = coef_ref[6, l] * u
            w = w + coef_ref[0, l] * pltpu.roll(u, window - 1, 0)
            w = w + coef_ref[1, l] * pltpu.roll(u, 1, 0)
            w = w + coef_ref[2, l] * pltpu.roll(u, lanes - 1, 1)
            w = w + coef_ref[3, l] * pltpu.roll(u, 1, 1)
            if l < levels - 1:
                w = w + coef_ref[4, l] * fields[l + 1]
            if l:
                w = w + coef_ref[5, l] * fields[l - 1]
            value = coef_ref[7, l] * w + coef_ref[8, l] * pltpu.roll(w, lc, 1)
            if l == 0:
                value = value + surface
            results.append(value)
        return results

    start_rows = gather_rows(rows, SECTIONS - HALO // COARSEN)

    def start_level(l):
        return dot(start_rows, dot(s_ref[0, l + 1], fold0) + dot(s_ref[1, l + 1], fold1))

    for l, value in enumerate(coarse_step(start_level)):
        value = jnp.where(inner, value, 0.0)
        first_ref[l] = value
        jump = o_ref[0, l] - value
        jump_ref[l] = jump
        low, high = halo_parts(jump)
        pl_ref[l] = low
        pr_ref[l] = high
    sends += [send(7, pl_ref, jl_ref, tm, right), send(8, pr_ref, jr_ref, tm, left)]

    sends[4].wait_recv()
    sends[5].wait_recv()
    sends[6].wait_recv()

    def widened(value, low, high):
        return jnp.concatenate([value[:8] + low, value[8:window - 8], value[window - 8:] + high], 0)

    for section in range(SECTIONS):
        if section:
            sends[8 + section].wait_recv()
        if section == 0:
            results = coarse_step(lambda l: widened(x_ref[0, l], xl_ref[l], xr_ref[l]))
            sends[7].wait_recv()
            sends[8].wait_recv()
            for l in range(levels):
                jump_ref[l] = widened(jump_ref[l], jl_ref[l], jr_ref[l])
        else:
            results = coarse_step(lambda l: x_ref[section, l])
        for l in range(levels):
            if section < SECTIONS - 1:
                o_ref[section + 1, l] = results[l] + jump_ref[l]
            else:
                o_ref[section + 1, l] = results[l] - first_ref[l]
        sends.append(send(9 + section, o_ref.at[section + 1], x_ref.at[section + 1], after, space))
        if section < SECTIONS - 1:
            send_chunk(section + 1)

    spread_rows = jnp.where(
        iota((nf, window), 0) // COARSEN + SECTIONS == iota((nf, window), 1), 1.0, 0.0
    )
    spread0 = jnp.where(iota((lanes, lat), 1) // COARSEN == iota((lanes, lat), 0), 1.0, 0.0)
    spread1 = jnp.where(iota((lanes, lat), 1) // COARSEN + lc == iota((lanes, lat), 0), 1.0, 0.0)
    for copy in big:
        copy.wait_recv()
    sends[-1].wait_recv()
    for l in range(levels):
        value = dot(spread_rows, x_ref[SECTIONS, l])
        out_ref[0, 0, l] = got_ref[0, l] + dot(value, spread0)
        out_ref[0, 1, l] = got_ref[1, l] + dot(value, spread1)
    for copy in sends + big:
        copy.wait_send()


def shards(start_states, wet_levels, advection, forcing, rates):
    _, tracers, levels, nf, lat = start_states.shape
    nc = nf // COARSEN
    lanes = 2 * (lat // COARSEN)
    window = -(-(nc + 2 * SECTIONS) // 8) * 8
    rows = nf + 2 * HALO
    year = STEPS * lax.axis_size("tm")
    segment = lax.axis_index("tm").astype(jnp.float32)
    offsets = jnp.array([step + 0.5 for step in range(STEPS)] + [STEPS * 0.5], jnp.float32)
    seasons = season_at(segment * STEPS + offsets, year)
    f32 = jnp.float32
    state = pltpu.VMEM((tracers, levels + 2, rows, lat), f32)
    ended = pltpu.VMEM((tracers, levels, nf, lat), f32)
    coarse = pltpu.VMEM((levels, window, lanes), f32)
    edge = pltpu.VMEM((levels, 8, lanes), f32)
    shifts = pltpu.VMEM((SECTIONS + 1, levels, window, lanes), f32)
    copies = 13 + SECTIONS
    vmem = pl.BlockSpec(memory_space=pltpu.VMEM)
    smem = pl.BlockSpec(memory_space=pltpu.SMEM)
    return pl.pallas_call(
        kernel,
        out_shape=jax.ShapeDtypeStruct(start_states.shape, f32),
        in_specs=[pl.BlockSpec(memory_space=pl.ANY), vmem, vmem, vmem, smem, smem],
        out_specs=vmem,
        scratch_shapes=[
            state, state, state, ended, ended,
            pltpu.VMEM((levels, rows, lat), f32),
            pltpu.VMEM((3, nf + 2 * WIDE, lat), f32),
            pltpu.VMEM((9, levels, window, lanes), f32),
            coarse, coarse, shifts, edge, edge, edge, edge,
            shifts, edge, edge, edge, edge,
            pltpu.SemaphoreType.DMA(()),
            pltpu.SemaphoreType.DMA((copies,)),
            pltpu.SemaphoreType.DMA((copies,)),
        ],
        compiler_params=pltpu.CompilerParams(
            collective_id=0, has_side_effects=True, vmem_limit_bytes=48 * 1024 * 1024
        ),
    )(start_states, wet_levels, advection, forcing, rates, seasons)


def solution(mesh):
    return jax.shard_map(
        shards,
        mesh=mesh,
        in_specs=(
            P("tm", None, None, "space", None),
            P("space", None),
            P("space", None),
            P("space", None),
            P(),
        ),
        out_specs=P("tm", None, None, "space", None),
        check_vma=False,
    )
```

```python
import math

import jax
import jax.numpy as jnp
from jax import lax
from jax.experimental import pallas as pl
from jax.experimental.pallas import tpu as pltpu
from jax.sharding import PartitionSpec as P

STEPS = 4
SECTIONS = 4
COARSEN = 4
RELAX = 0.2
HALO = 8
WIDE = COARSEN * SECTIONS
MESH = pl.DeviceIdType.MESH


def season_at(position, year):
    return 1.0 + 0.6 * jnp.sin(2.0 * math.pi * position / year)


def iota(shape, dim):
    return lax.broadcasted_iota(jnp.int32, shape, dim)


def dot(a, b):
    return jnp.dot(a, b, preferred_element_type=jnp.float32)


def split(value):
    parts = []
    for _ in range(3):
        part = value.astype(jnp.bfloat16)
        value = value - part.astype(jnp.float32)
        parts.append(part)
    return parts


def exact(flags, value):
    return jnp.where(flags, value, 0.0).astype(jnp.bfloat16)


def fold_rows(weights, value):
    return dot(jnp.concatenate([weights] * 3, 1), jnp.concatenate(split(value), 0))


def kernel(
    start_ref, wet_hbm, flow_hbm, forcing_hbm, rates_hbm, out_ref,
    s_ref, a_ref, b_ref, end_ref, got_ref, diag_ref, aux_ref,
    coef_ref, first_ref, jump_ref, x_ref, xl_ref, xr_ref, jl_ref, jr_ref,
    o_ref, ol_ref, or_ref, pl_ref, pr_ref,
    wet_ref, rates_ref, local_sem, send_sem, recv_sem,
):
    tracers, levels, nf, lat = end_ref.shape
    nc = nf // COARSEN
    lc = lat // COARSEN
    lanes = 2 * lc
    window = coef_ref.shape[2]
    rows = nf + 2 * HALO
    tm, n_tm = lax.axis_index("tm"), lax.axis_size("tm")
    space, n_space = lax.axis_index("space"), lax.axis_size("space")
    after, before = lax.rem(tm + 1, n_tm), lax.rem(tm + n_tm - 1, n_tm)
    right, left = lax.rem(space + 1, n_space), lax.rem(space + n_space - 1, n_space)

    barrier = pltpu.get_barrier_semaphore()
    for i, j in ((tm, left), (tm, right), (before, space), (before, left), (before, right)):
        pl.semaphore_signal(barrier, inc=1, device_id=(i, j), device_id_type=MESH)

    mid = pl.ds(WIDE, nf)
    loads = [
        pltpu.make_async_copy(src, dst, local_sem.at[i])
        for i, (src, dst) in enumerate((
            (wet_hbm, wet_ref),
            (flow_hbm, aux_ref.at[1, mid, :]),
            (forcing_hbm, aux_ref.at[2, mid, :]),
            (rates_hbm, rates_ref),
            (start_ref.at[0], s_ref.at[:, pl.ds(1, levels), pl.ds(HALO, nf), :]),
        ))
    ]
    for load in loads:
        load.start()
    where = jnp.minimum(iota((8, 128), 1).astype(jnp.float32) + 0.5, STEPS + 0.5)
    where = jnp.where(where > STEPS, STEPS * 0.5, where)
    begin = (tm * STEPS).astype(jnp.float32)
    season_ref = season_at(begin + where, STEPS * n_tm)
    zero = jnp.zeros((tracers, rows, lat), jnp.float32)
    for ref in (s_ref, a_ref, b_ref):
        ref[:, 0] = zero
        ref[:, levels + 1] = zero
    for load in loads[:3]:
        load.wait()
    aux_ref[0, mid, :] = wet_ref[...].astype(jnp.float32)
    pl.semaphore_wait(barrier, 5)

    def send(index, src, dst, i, j):
        copy = pltpu.make_async_remote_copy(
            src_ref=src, dst_ref=dst, send_sem=send_sem.at[index], recv_sem=recv_sem.at[index],
            device_id=(i, j), device_id_type=MESH,
        )
        copy.start()
        return copy

    sends = [
        send(0, aux_ref.at[:, pl.ds(nf, WIDE), :], aux_ref.at[:, pl.ds(0, WIDE), :], tm, right),
        send(1, aux_ref.at[:, pl.ds(WIDE, WIDE), :],
             aux_ref.at[:, pl.ds(WIDE + nf, WIDE), :], tm, left),
        send(2, start_ref.at[0, :, :, pl.ds(nf - HALO, HALO), :],
             s_ref.at[:, pl.ds(1, levels), pl.ds(0, HALO), :], tm, right),
        send(3, start_ref.at[0, :, :, pl.ds(0, HALO), :],
             s_ref.at[:, pl.ds(1, levels), pl.ds(HALO + nf, HALO), :], tm, left),
    ]

    loads[3].wait()
    sends[0].wait_recv()
    sends[1].wait_recv()
    fine = pl.ds(WIDE - HALO, rows)
    wide = aux_ref[0, fine, :]
    lane = iota((rows, lat), 1)
    wet_e = pltpu.roll(wide, rows - 1, 0)
    wet_w = pltpu.roll(wide, 1, 0)
    wet_n = jnp.where(lane == lat - 1, 0.0, pltpu.roll(wide, lat - 1, 1))
    wet_s = jnp.where(lane == 0, 0.0, pltpu.roll(wide, 1, 1))
    flow = aux_ref[1, fine, :]
    for l in range(levels):
        k = rates_ref[0, l]
        west = jnp.where(wet_w > l, 1.0, 0.0)
        count = west
        for other in (wet_e, wet_n, wet_s):
            count = count + jnp.where(other > l, 1.0, 0.0)
        total = 1.0 - k * count - flow * west
        if l:
            total = total - rates_ref[1, l - 1]
        if l < levels - 1:
            total = total - jnp.where(wide > l + 1, rates_ref[1, l], 0.0)
        diag_ref[l] = total
    quarter = 1.0 / COARSEN
    group, folded = iota((lat, lanes), 0) // COARSEN, iota((lat, lanes), 1)
    fold0 = exact(group == folded, quarter)
    fold1 = exact(group + lc == folded, quarter)
    both = fold0 + fold1

    def gather_rows(count, base):
        shape = (window, count)
        return exact(iota(shape, 1) // COARSEN + base == iota(shape, 0), quarter)

    def fold_lat(nutrient, organic):
        pairs = zip(split(nutrient), split(organic))
        return sum(dot(first, fold0) + dot(second, fold1) for first, second in pairs)

    row = iota((window, lanes), 0)
    col = iota((window, lanes), 1)
    inner = (row >= SECTIONS) & (row < SECTIONS + nc)
    to_right = iota((8, lanes), 0) < SECTIONS
    tail = iota((8, lanes), 0) + (window - 8)
    to_left = (tail >= SECTIONS + nc) & (tail < 2 * SECTIONS + nc)

    wide_rows = gather_rows(nf + 2 * WIDE, 0)
    c_flow = fold_rows(wide_rows, fold_lat(aux_ref[1], aux_ref[1])) * (STEPS / COARSEN)
    c_forcing = fold_rows(wide_rows, fold_lat(aux_ref[2], aux_ref[2]))
    wet = aux_ref[0]
    masks = [
        dot(wide_rows, dot(exact(wet > l, 1.0), both).astype(jnp.bfloat16)) for l in range(levels)
    ]
    season = season_ref[0, STEPS]
    is_nutrient = col < lc
    edge_n = (col == lc - 1) | (col == lanes - 1)
    edge_s = (col == 0) | (col == lc)
    for l in range(levels):
        m = masks[l]
        k = rates_ref[0, l] * (STEPS / COARSEN**2)
        g = rates_ref[2, l] * STEPS * season
        r = rates_ref[3, l] * STEPS
        q = RELAX * STEPS if l == 0 else 0.0
        m_w = pltpu.roll(m, 1, 0)
        east = k * pltpu.roll(m, window - 1, 0)
        west = (k + c_flow) * m_w
        north = k * jnp.where(edge_n, 0.0, pltpu.roll(m, lanes - 1, 1))
        south = k * jnp.where(edge_s, 0.0, pltpu.roll(m, 1, 1))
        total = 1.0 - east - west - north - south
        if l < levels - 1:
            down = rates_ref[1, l] * STEPS * masks[l + 1]
            total = total - down
            coef_ref[4, l] = down
        if l:
            up = rates_ref[1, l - 1] * STEPS * masks[l - 1]
            total = total - up
            coef_ref[5, l] = up
        coef_ref[0, l] = east
        coef_ref[1, l] = west
        coef_ref[2, l] = north
        coef_ref[3, l] = south
        coef_ref[6, l] = total
        coef_ref[7, l] = m * jnp.where(is_nutrient, 1.0 - g - q, 1.0 - r)
        coef_ref[8, l] = m * jnp.where(is_nutrient, r, g)
    surface = masks[0] * jnp.where(is_nutrient, RELAX * STEPS * c_forcing, 0.0)

    loads[4].wait()
    sends[2].wait_recv()
    sends[3].wait_recv()

    def fine_step(src, dst, step):
        season = season_ref[0, step]

        def level(l, carry):
            k, v, g, r = (rates_ref[i, l] for i in range(4))
            upper = rates_ref[1, lax.rem(l + levels - 1, levels)]
            lf = l.astype(jnp.float32)
            wet = aux_ref[0, fine, :]
            here = wet > lf
            speed = aux_ref[1, fine, :] + k
            centre = diag_ref[l]
            lane = iota((rows, lat), 1)
            mixed = []
            for t in range(tracers):
                u = src[t, l + 1]
                up = src[t, l]
                down = src[t, l + 2]
                if step == 0:
                    u = jnp.where(here, u, 0.0)
                    up = jnp.where(wet > lf - 1.0, up, 0.0)
                    down = jnp.where(wet > lf + 1.0, down, 0.0)
                east = pltpu.roll(u, rows - 1, 0)
                west = pltpu.roll(u, 1, 0)
                north = jnp.where(lane == lat - 1, 0.0, pltpu.roll(u, lat - 1, 1))
                south = jnp.where(lane == 0, 0.0, pltpu.roll(u, 1, 1))
                mixed.append(
                    centre * u + k * (east + north + south) + speed * west + v * down + upper * up
                )
            grown = g * season
            q = jnp.where(l == 0, RELAX, 0.0)
            nutrient = mixed[0] * (1.0 - grown - q) + r * mixed[1] + q * aux_ref[2, fine, :]
            organic = mixed[1] * (1.0 - r) + grown * mixed[0]
            nutrient = jnp.where(here, nutrient, 0.0)
            organic = jnp.where(here, organic, 0.0)
            if step < STEPS - 1:
                dst[0, l + 1] = nutrient
                dst[1, l + 1] = organic
            else:
                dst[0, l] = nutrient[HALO:HALO + nf]
                dst[1, l] = organic[HALO:HALO + nf]
            return carry

        lax.fori_loop(0, levels, level, 0)

    fine_step(s_ref, a_ref, 0)
    fine_step(a_ref, b_ref, 1)
    fine_step(b_ref, a_ref, 2)
    fine_step(a_ref, end_ref, 3)

    def halo_parts(value):
        low = jnp.where(to_right, pltpu.roll(value, window - nc, 0)[:8], 0.0)
        high = jnp.where(to_left, pltpu.roll(value, nc, 0)[window - 8:], 0.0)
        return low, high

    centre_rows = gather_rows(nf, SECTIONS)
    chunk = levels // SECTIONS
    flat = (chunk * nf, lat)
    for c in range(SECTIONS):
        part = pl.ds(c * chunk, chunk)
        folds = fold_lat(end_ref[0, part].reshape(flat), end_ref[1, part].reshape(flat))
        for j in range(chunk):
            l = c * chunk + j
            value = fold_rows(centre_rows, folds[j * nf:(j + 1) * nf])
            o_ref[0, l] = value
            low, high = halo_parts(value)
            ol_ref[l] = low
            or_ref[l] = high
    sends += [
        send(4, o_ref.at[0], x_ref.at[0], after, space),
        send(5, ol_ref, xl_ref, after, right),
        send(6, or_ref, xr_ref, after, left),
    ]
    big = []

    def send_chunk(index):
        part = pl.ds(index * chunk, chunk)
        big.append(send(13 + index, end_ref.at[:, part], got_ref.at[:, part], after, space))

    send_chunk(0)

    def coarse_step(load_level):
        fields = [load_level(l) for l in range(levels)]
        results = []
        for l in range(levels):
            u = fields[l]
            w = coef_ref[6, l] * u
            w = w + coef_ref[0, l] * pltpu.roll(u, window - 1, 0)
            w = w + coef_ref[1, l] * pltpu.roll(u, 1, 0)
            w = w + coef_ref[2, l] * pltpu.roll(u, lanes - 1, 1)
            w = w + coef_ref[3, l] * pltpu.roll(u, 1, 1)
            if l < levels - 1:
                w = w + coef_ref[4, l] * fields[l + 1]
            if l:
                w = w + coef_ref[5, l] * fields[l - 1]
            value = coef_ref[7, l] * w + coef_ref[8, l] * pltpu.roll(w, lc, 1)
            if l == 0:
                value = value + surface
            results.append(value)
        return results

    start_rows = gather_rows(rows, SECTIONS - HALO // COARSEN)

    restricted = []
    flat = (chunk * rows, lat)
    for c in range(SECTIONS):
        part = pl.ds(1 + c * chunk, chunk)
        folds = fold_lat(s_ref[0, part].reshape(flat), s_ref[1, part].reshape(flat))
        for j in range(chunk):
            restricted.append(fold_rows(start_rows, folds[j * rows:(j + 1) * rows]))

    for l, value in enumerate(coarse_step(lambda l: restricted[l])):
        value = jnp.where(inner, value, 0.0)
        first_ref[l] = value
        jump = o_ref[0, l] - value
        jump_ref[l] = jump
        low, high = halo_parts(jump)
        pl_ref[l] = low
        pr_ref[l] = high
    sends += [send(7, pl_ref, jl_ref, tm, right), send(8, pr_ref, jr_ref, tm, left)]

    sends[4].wait_recv()
    sends[5].wait_recv()
    sends[6].wait_recv()

    def widened(value, low, high):
        return jnp.concatenate([value[:8] + low, value[8:window - 8], value[window - 8:] + high], 0)

    for section in range(SECTIONS):
        if section:
            sends[8 + section].wait_recv()
        if section == 0:
            results = coarse_step(lambda l: widened(x_ref[0, l], xl_ref[l], xr_ref[l]))
            sends[7].wait_recv()
            sends[8].wait_recv()
            for l in range(levels):
                jump_ref[l] = widened(jump_ref[l], jl_ref[l], jr_ref[l])
        else:
            results = coarse_step(lambda l: x_ref[section, l])
        for l in range(levels):
            if section < SECTIONS - 1:
                o_ref[section + 1, l] = results[l] + jump_ref[l]
            else:
                o_ref[section + 1, l] = results[l] - first_ref[l]
        sends.append(send(9 + section, o_ref.at[section + 1], x_ref.at[section + 1], after, space))
        if section < SECTIONS - 1:
            send_chunk(section + 1)

    shape = (nf, window)
    spread_rows = exact(iota(shape, 0) // COARSEN + SECTIONS == iota(shape, 1), 1.0)
    shape = (lanes, lat)
    group = iota(shape, 1) // COARSEN
    spread0 = exact(group == iota(shape, 0), 1.0)
    spread1 = exact(group + lc == iota(shape, 0), 1.0)
    for copy in big:
        copy.wait_recv()
    sends[-1].wait_recv()
    for c in range(SECTIONS):
        stacked = []
        for l in range(c * chunk, (c + 1) * chunk):
            stacked.append([
                dot(spread_rows, part).astype(jnp.bfloat16) for part in split(x_ref[SECTIONS, l])
            ])
        parts = [jnp.concatenate(same, 0) for same in zip(*stacked)]
        for t, spread in enumerate((spread0, spread1)):
            value = sum(dot(part, spread) for part in parts).reshape(chunk, nf, lat)
            part = pl.ds(c * chunk, chunk)
            out_ref[0, t, part] = got_ref[t, part] + value
    for copy in sends + big:
        copy.wait_send()


def shards(start_states, wet_levels, advection, forcing, rates):
    _, tracers, levels, nf, lat = start_states.shape
    nc = nf // COARSEN
    lanes = 2 * (lat // COARSEN)
    window = -(-(nc + 2 * SECTIONS) // 8) * 8
    rows = nf + 2 * HALO
    f32 = jnp.float32
    state = pltpu.VMEM((tracers, levels + 2, rows, lat), f32)
    ended = pltpu.VMEM((tracers, levels, nf, lat), f32)
    coarse = pltpu.VMEM((levels, window, lanes), f32)
    edge = pltpu.VMEM((levels, 8, lanes), f32)
    shifts = pltpu.VMEM((SECTIONS + 1, levels, window, lanes), f32)
    copies = 13 + SECTIONS
    vmem = pl.BlockSpec(memory_space=pltpu.VMEM)
    hbm = pl.BlockSpec(memory_space=pltpu.HBM)
    return pl.pallas_call(
        kernel,
        out_shape=jax.ShapeDtypeStruct(start_states.shape, f32),
        in_specs=[hbm] * 5,
        out_specs=vmem,
        scratch_shapes=[
            state, state, state, ended, ended,
            pltpu.VMEM((levels, rows, lat), f32),
            pltpu.VMEM((3, nf + 2 * WIDE, lat), f32),
            pltpu.VMEM((9, levels, window, lanes), f32),
            coarse, coarse, shifts, edge, edge, edge, edge,
            shifts, edge, edge, edge, edge,
            pltpu.VMEM((nf, lat), jnp.int32),
            pltpu.SMEM(rates.shape, f32),
            pltpu.SemaphoreType.DMA((5,)),
            pltpu.SemaphoreType.DMA((copies,)),
            pltpu.SemaphoreType.DMA((copies,)),
        ],
        compiler_params=pltpu.CompilerParams(
            collective_id=0, has_side_effects=True, vmem_limit_bytes=64 * 1024 * 1024
        ),
    )(start_states, wet_levels, advection, forcing, rates)


def solution(mesh):
    return jax.shard_map(
        shards,
        mesh=mesh,
        in_specs=(
            P("tm", None, None, "space", None),
            P("space", None),
            P("space", None),
            P("space", None),
            P(),
        ),
        out_specs=P("tm", None, None, "space", None),
        check_vma=False,
    )
```

```python
import math

import jax
import jax.numpy as jnp
from jax import lax
from jax.experimental import pallas as pl
from jax.experimental.pallas import tpu as pltpu
from jax.sharding import PartitionSpec as P

STEPS = 4
SECTIONS = 4
COARSEN = 4
RELAX = 0.2
EDGE = 8
LANES = 128
CHUNK = 2
WIDE = COARSEN * SECTIONS
MESH = pl.DeviceIdType.MESH


def season_at(position, year):
    return 1.0 + 0.6 * jnp.sin(2.0 * math.pi * position / year)


def iota(shape, dim):
    return lax.broadcasted_iota(jnp.int32, shape, dim)


def dot(a, b):
    return jnp.dot(a, b, preferred_element_type=jnp.float32)


def split(value):
    parts = []
    for _ in range(3):
        part = value.astype(jnp.bfloat16)
        value = value - part.astype(jnp.float32)
        parts.append(part)
    return parts


def exact(flags, value):
    return jnp.where(flags, value, 0.0).astype(jnp.bfloat16)


def fold_rows(weights, value):
    if weights.shape[1] > value.shape[0]:
        rest = weights.shape[1] - value.shape[0]
        value = jnp.concatenate([value, jnp.zeros((rest, value.shape[1]), value.dtype)], 0)
    return dot(jnp.concatenate([weights] * 3, 1), jnp.concatenate(split(value), 0))


def kernel(
    start_ref, wet_hbm, flow_hbm, forcing_hbm, rates_hbm, out_ref,
    s_ref, state_ref, ring_ref, diag_ref, aux_ref, edge_ref, pack_ref, hr_ref, hl_ref,
    coef_ref, first_ref, jump_ref, x_ref, xl_ref, xr_ref, jl_ref, jr_ref,
    o_ref, ol_ref, or_ref, pl_ref, pr_ref,
    wet_ref, rates_ref, local_sem, send_sem, recv_sem,
):
    _, tracers, levels, nf, lat = out_ref.shape
    nc = nf // COARSEN
    lc = lat // COARSEN
    lanes = 2 * lc
    window = coef_ref.shape[2]
    rows = nf + EDGE
    tm, n_tm = lax.axis_index("tm"), lax.axis_size("tm")
    space, n_space = lax.axis_index("space"), lax.axis_size("space")
    after, before = lax.rem(tm + 1, n_tm), lax.rem(tm + n_tm - 1, n_tm)
    right, left = lax.rem(space + 1, n_space), lax.rem(space + n_space - 1, n_space)

    barrier = pltpu.get_barrier_semaphore()
    for i, j in ((tm, left), (tm, right), (before, space), (before, left), (before, right)):
        pl.semaphore_signal(barrier, inc=1, device_id=(i, j), device_id_type=MESH)

    mid = pl.ds(WIDE, nf)
    loads = [
        pltpu.make_async_copy(src, dst, local_sem.at[i])
        for i, (src, dst) in enumerate((
            (wet_hbm, wet_ref),
            (flow_hbm, aux_ref.at[1, mid, :]),
            (forcing_hbm, aux_ref.at[2, mid, :]),
            (rates_hbm, rates_ref),
            (start_ref.at[0, :, :, pl.ds(0, EDGE), :], edge_ref.at[0]),
            (start_ref.at[0, :, :, pl.ds(nf - EDGE, EDGE), :], edge_ref.at[1]),
        ))
    ]
    for load in loads:
        load.start()
    where = jnp.minimum(iota((8, 128), 1).astype(jnp.float32) + 0.5, STEPS + 0.5)
    where = jnp.where(where > STEPS, STEPS * 0.5, where)
    begin = (before * STEPS).astype(jnp.float32)
    season_ref = season_at(begin + where, STEPS * n_tm)
    zero = jnp.zeros((tracers, rows, lat), jnp.float32)
    for step in range(STEPS):
        state_ref[step, :, 0] = zero
        state_ref[step, :, levels + 1] = zero
    for load in loads[:3]:
        load.wait()
    aux_ref[0, mid, :] = wet_ref[...].astype(jnp.float32)
    loads[4].wait()
    loads[5].wait()
    upper_half = iota((EDGE, lat), 0) < COARSEN
    for l in range(levels):
        pack_ref[0, l] = jnp.where(
            upper_half, edge_ref[0, 0, l], pltpu.roll(edge_ref[0, 1, l], COARSEN, 0)
        )
        pack_ref[1, l] = jnp.where(
            upper_half, pltpu.roll(edge_ref[1, 0, l], COARSEN, 0), edge_ref[1, 1, l]
        )
    pl.semaphore_wait(barrier, 5)

    def send(index, src, dst, i, j):
        copy = pltpu.make_async_remote_copy(
            src_ref=src, dst_ref=dst, send_sem=send_sem.at[index], recv_sem=recv_sem.at[index],
            device_id=(i, j), device_id_type=MESH,
        )
        copy.start()
        return copy

    sends = [
        send(0, aux_ref.at[:, pl.ds(nf, WIDE), :], aux_ref.at[:, pl.ds(0, WIDE), :], tm, right),
        send(1, aux_ref.at[:, pl.ds(WIDE, WIDE), :],
             aux_ref.at[:, pl.ds(WIDE + nf, WIDE), :], tm, left),
        send(2, pack_ref.at[0], hr_ref, after, left),
        send(3, pack_ref.at[1], hl_ref, after, right),
    ]

    def piece(index):
        part = pl.ds(index * CHUNK, CHUNK)
        return pltpu.make_async_remote_copy(
            src_ref=start_ref.at[0, :, part], dst_ref=s_ref.at[:, part, pl.ds(0, nf), :],
            send_sem=send_sem.at[12 + index], recv_sem=recv_sem.at[12 + index],
            device_id=(after, space), device_id_type=MESH,
        )

    pieces = levels // CHUNK
    for index in range(pieces):
        piece(index).start()

    loads[3].wait()
    sends[0].wait_recv()
    sends[1].wait_recv()
    half = iota((EDGE, lat), 0) < COARSEN
    for i in range(3):
        ring_ref[i, pl.ds(0, nf), :] = aux_ref[i, mid, :]
        ring_ref[i, pl.ds(nf, EDGE), :] = jnp.where(
            half, aux_ref[i, pl.ds(WIDE + nf, EDGE), :], aux_ref[i, pl.ds(WIDE - EDGE, EDGE), :]
        )
    wide = ring_ref[0]
    lane = iota((rows, lat), 1)
    wet_e = pltpu.roll(wide, rows - 1, 0)
    wet_w = pltpu.roll(wide, 1, 0)
    wet_n = jnp.where(lane == lat - 1, 0.0, pltpu.roll(wide, lat - 1, 1))
    wet_s = jnp.where(lane == 0, 0.0, pltpu.roll(wide, 1, 1))
    flow = ring_ref[1]
    for l in range(levels):
        k = rates_ref[0, l]
        west = jnp.where(wet_w > l, 1.0, 0.0)
        count = west
        for other in (wet_e, wet_n, wet_s):
            count = count + jnp.where(other > l, 1.0, 0.0)
        total = 1.0 - k * count - flow * west
        if l:
            total = total - rates_ref[1, l - 1]
        if l < levels - 1:
            total = total - jnp.where(wide > l + 1, rates_ref[1, l], 0.0)
        diag_ref[l] = total
    quarter = 1.0 / COARSEN
    group, folded = iota((lat, lanes), 0) // COARSEN, iota((lat, lanes), 1)
    fold0 = exact(group == folded, quarter)
    fold1 = exact(group + lc == folded, quarter)
    both = fold0 + fold1

    def gather_rows(count, base):
        shape = (window, count)
        return exact(iota(shape, 1) // COARSEN + base == iota(shape, 0), quarter)

    def fold_lat(nutrient, organic):
        pairs = zip(split(nutrient), split(organic))
        return sum(dot(first, fold0) + dot(second, fold1) for first, second in pairs)

    row = iota((window, lanes), 0)
    col = iota((window, lanes), 1)
    inner = (row >= SECTIONS) & (row < SECTIONS + nc)
    to_right = iota((8, lanes), 0) < SECTIONS
    tail = iota((8, lanes), 0) + (window - 8)
    to_left = (tail >= SECTIONS + nc) & (tail < 2 * SECTIONS + nc)

    wide_rows = gather_rows(nf + 2 * WIDE, 0)
    c_flow = fold_rows(wide_rows, fold_lat(aux_ref[1], aux_ref[1])) * (STEPS / COARSEN)
    c_forcing = fold_rows(wide_rows, fold_lat(aux_ref[2], aux_ref[2]))
    wet = aux_ref[0]
    masks = [
        dot(wide_rows, dot(exact(wet > l, 1.0), both).astype(jnp.bfloat16)) for l in range(levels)
    ]
    season = season_ref[0, STEPS]
    is_nutrient = col < lc
    edge_n = (col == lc - 1) | (col == lanes - 1)
    edge_s = (col == 0) | (col == lc)
    for l in range(levels):
        m = masks[l]
        k = rates_ref[0, l] * (STEPS / COARSEN**2)
        g = rates_ref[2, l] * STEPS * season
        r = rates_ref[3, l] * STEPS
        q = RELAX * STEPS if l == 0 else 0.0
        m_w = pltpu.roll(m, 1, 0)
        east = k * pltpu.roll(m, window - 1, 0)
        west = (k + c_flow) * m_w
        north = k * jnp.where(edge_n, 0.0, pltpu.roll(m, lanes - 1, 1))
        south = k * jnp.where(edge_s, 0.0, pltpu.roll(m, 1, 1))
        total = 1.0 - east - west - north - south
        if l < levels - 1:
            down = rates_ref[1, l] * STEPS * masks[l + 1]
            total = total - down
            coef_ref[4, l] = down
        if l:
            up = rates_ref[1, l - 1] * STEPS * masks[l - 1]
            total = total - up
            coef_ref[5, l] = up
        coef_ref[0, l] = east
        coef_ref[1, l] = west
        coef_ref[2, l] = north
        coef_ref[3, l] = south
        coef_ref[6, l] = total
        coef_ref[7, l] = m * jnp.where(is_nutrient, 1.0 - g - q, 1.0 - r)
        coef_ref[8, l] = m * jnp.where(is_nutrient, r, g)
    surface = masks[0] * jnp.where(is_nutrient, RELAX * STEPS * c_forcing, 0.0)

    sends[2].wait_recv()
    sends[3].wait_recv()
    padded_rows = -(-rows // 16) * 16
    at, ring = iota((window, padded_rows), 0), iota((window, padded_rows), 1)
    start_rows = exact(
        ((ring < nf + COARSEN) & (ring // COARSEN + SECTIONS == at))
        | ((ring >= nf + COARSEN) & (ring < rows) & (at == SECTIONS - 1)),
        quarter,
    )

    def arrive(index):
        piece(index).wait_recv()
        part = pl.ds(index * CHUNK, CHUNK)
        for j in range(CHUNK):
            l = index * CHUNK + j
            high, low = hr_ref[l], hl_ref[l]
            s_ref[0, l, pl.ds(nf, EDGE), :] = jnp.where(half, high, pltpu.roll(low, COARSEN, 0))
            s_ref[1, l, pl.ds(nf, EDGE), :] = jnp.where(half, pltpu.roll(high, COARSEN, 0), low)
            here = ring_ref[0] > jnp.asarray(l, jnp.float32)
            for t in range(tracers):
                state_ref[0, t, l + 1] = jnp.where(here, s_ref[t, l], 0.0)
        flat = (CHUNK * rows, lat)
        folds = fold_lat(s_ref[0, part].reshape(flat), s_ref[1, part].reshape(flat))
        for j in range(CHUNK):
            value = fold_rows(start_rows, folds[j * rows:(j + 1) * rows])
            first_ref[index * CHUNK + j] = value

    sub = iota((EDGE, LANES), 0)
    lane = iota((EDGE, LANES), 1)
    blocks = rows // EDGE
    tiles = lat // LANES

    def fine_level(step, l):
        season = season_ref[0, step]
        k, v, g, r = (rates_ref[i, l] for i in range(4))
        upper = rates_ref[1, lax.rem(l + levels - 1, levels)]
        lf = l.astype(jnp.float32)
        grown = g * season
        q = jnp.where(l == 0, RELAX, 0.0)
        kept, stays = 1.0 - grown - q, 1.0 - r
        for x in range(tiles):
            across = pl.ds(x * LANES, LANES)
            cells, norths, souths = [], [], []
            for t in range(tracers):
                cell = [
                    state_ref[step, t, l + 1, pl.ds(b * EDGE, EDGE), across] for b in range(blocks)
                ]
                cells.append(
                    (cell, [pltpu.roll(c, EDGE - 1, 0) for c in cell],
                     [pltpu.roll(c, 1, 0) for c in cell])
                )
            for b in range(blocks if step < STEPS - 1 else blocks - 1):
                down_rows = pl.ds(b * EDGE, EDGE)
                centre = diag_ref[l, down_rows, across]
                speed = ring_ref[1, down_rows, across] + k
                here = ring_ref[0, down_rows, across] > lf
                mixed = []
                for t in range(tracers):
                    cell, fore, back = cells[t]
                    u = cell[b]
                    east = jnp.where(sub == EDGE - 1, fore[(b + 1) % blocks], fore[b])
                    west = jnp.where(sub == 0, back[(b + blocks - 1) % blocks], back[b])
                    if x + 1 < tiles:
                        ahead = state_ref[step, t, l + 1, down_rows, pl.ds((x + 1) * LANES, LANES)]
                        ahead = pltpu.roll(ahead, LANES - 1, 1)
                    else:
                        ahead = 0.0
                    if x:
                        behind = state_ref[step, t, l + 1, down_rows, pl.ds((x - 1) * LANES, LANES)]
                        behind = pltpu.roll(behind, 1, 1)
                    else:
                        behind = 0.0
                    north = jnp.where(lane == LANES - 1, ahead, pltpu.roll(u, LANES - 1, 1))
                    south = jnp.where(lane == 0, behind, pltpu.roll(u, 1, 1))
                    mixed.append(
                        centre * u + k * (east + north + south) + speed * west
                        + v * state_ref[step, t, l + 2, down_rows, across]
                        + upper * state_ref[step, t, l, down_rows, across]
                    )
                nutrient = mixed[0] * kept + r * mixed[1] + q * ring_ref[2, down_rows, across]
                organic = mixed[1] * stays + grown * mixed[0]
                nutrient = jnp.where(here, nutrient, 0.0)
                organic = jnp.where(here, organic, 0.0)
                if step < STEPS - 1:
                    state_ref[step + 1, 0, l + 1, down_rows, across] = nutrient
                    state_ref[step + 1, 1, l + 1, down_rows, across] = organic
                else:
                    out_ref[0, 0, l, down_rows, across] = nutrient
                    out_ref[0, 1, l, down_rows, across] = organic

    arrive(0)

    def diagonal(d, carry):
        @pl.when((lax.rem(d + 1, CHUNK) == 0) & (d + 1 < levels))
        def _():
            arrive((d + 1) // CHUNK)

        for step in range(STEPS):
            @pl.when((d >= step) & (d < levels + step))
            def _():
                fine_level(step, d - step)

        return carry

    lax.fori_loop(0, levels + STEPS - 1, diagonal, 0)

    def halo_parts(value):
        low = jnp.where(to_right, pltpu.roll(value, window - nc, 0)[:8], 0.0)
        high = jnp.where(to_left, pltpu.roll(value, nc, 0)[window - 8:], 0.0)
        return low, high

    centre_rows = gather_rows(nf, SECTIONS)
    chunk = levels // SECTIONS
    flat = (chunk * nf, lat)
    for c in range(SECTIONS):
        part = pl.ds(c * chunk, chunk)
        folds = fold_lat(out_ref[0, 0, part].reshape(flat), out_ref[0, 1, part].reshape(flat))
        for j in range(chunk):
            l = c * chunk + j
            value = fold_rows(centre_rows, folds[j * nf:(j + 1) * nf])
            o_ref[0, l] = value
            low, high = halo_parts(value)
            ol_ref[l] = low
            or_ref[l] = high
    sends += [
        send(4, o_ref.at[0], x_ref.at[0], after, space),
        send(5, ol_ref, xl_ref, after, right),
        send(6, or_ref, xr_ref, after, left),
    ]
    def coarse_step(load_level):
        fields = [load_level(l) for l in range(levels)]
        results = []
        for l in range(levels):
            u = fields[l]
            w = coef_ref[6, l] * u
            w = w + coef_ref[0, l] * pltpu.roll(u, window - 1, 0)
            w = w + coef_ref[1, l] * pltpu.roll(u, 1, 0)
            w = w + coef_ref[2, l] * pltpu.roll(u, lanes - 1, 1)
            w = w + coef_ref[3, l] * pltpu.roll(u, 1, 1)
            if l < levels - 1:
                w = w + coef_ref[4, l] * fields[l + 1]
            if l:
                w = w + coef_ref[5, l] * fields[l - 1]
            value = coef_ref[7, l] * w + coef_ref[8, l] * pltpu.roll(w, lc, 1)
            if l == 0:
                value = value + surface
            results.append(value)
        return results

    for l, value in enumerate(coarse_step(lambda l: first_ref[l])):
        value = jnp.where(inner, value, 0.0)
        first_ref[l] = value
        jump = o_ref[0, l] - value
        jump_ref[l] = jump
        low, high = halo_parts(jump)
        pl_ref[l] = low
        pr_ref[l] = high
    sends += [send(7, pl_ref, jl_ref, tm, right), send(8, pr_ref, jr_ref, tm, left)]

    sends[4].wait_recv()
    sends[5].wait_recv()
    sends[6].wait_recv()

    def widened(value, low, high):
        return jnp.concatenate([value[:8] + low, value[8:window - 8], value[window - 8:] + high], 0)

    for section in range(SECTIONS):
        if section:
            sends[8 + section].wait_recv()
        if section == 0:
            results = coarse_step(lambda l: widened(x_ref[0, l], xl_ref[l], xr_ref[l]))
            sends[7].wait_recv()
            sends[8].wait_recv()
            for l in range(levels):
                jump_ref[l] = widened(jump_ref[l], jl_ref[l], jr_ref[l])
        else:
            results = coarse_step(lambda l: x_ref[section, l])
        if section < SECTIONS - 1:
            for l in range(levels):
                o_ref[section + 1, l] = results[l] + jump_ref[l]
            sends.append(
                send(9 + section, o_ref.at[section + 1], x_ref.at[section + 1], after, space)
            )

    shape = (nf, window)
    spread_rows = exact(iota(shape, 0) // COARSEN + SECTIONS == iota(shape, 1), 1.0)
    shape = (lanes, lat)
    group = iota(shape, 1) // COARSEN
    spread0 = exact(group == iota(shape, 0), 1.0)
    spread1 = exact(group + lc == iota(shape, 0), 1.0)
    for c in range(SECTIONS):
        stacked = []
        for l in range(c * chunk, (c + 1) * chunk):
            stacked.append([
                dot(spread_rows, part).astype(jnp.bfloat16) for part in split(results[l] - first_ref[l])
            ])
        parts = [jnp.concatenate(same, 0) for same in zip(*stacked)]
        for t, spread in enumerate((spread0, spread1)):
            value = sum(dot(part, spread) for part in parts).reshape(chunk, nf, lat)
            part = pl.ds(c * chunk, chunk)
            out_ref[0, t, part] = out_ref[0, t, part] + value
    for copy in sends:
        copy.wait_send()
    for index in range(pieces):
        piece(index).wait_send()


def shards(start_states, wet_levels, advection, forcing, rates):
    _, tracers, levels, nf, lat = start_states.shape
    nc = nf // COARSEN
    lanes = 2 * (lat // COARSEN)
    window = -(-(nc + 2 * SECTIONS) // 8) * 8
    rows = nf + EDGE
    f32 = jnp.float32
    packed = pltpu.VMEM((levels, EDGE, lat), f32)
    coarse = pltpu.VMEM((levels, window, lanes), f32)
    edge = pltpu.VMEM((levels, 8, lanes), f32)
    shifts = pltpu.VMEM((SECTIONS, levels, window, lanes), f32)
    copies = 12 + levels // CHUNK
    vmem = pl.BlockSpec(memory_space=pltpu.VMEM)
    hbm = pl.BlockSpec(memory_space=pltpu.HBM)
    return pl.pallas_call(
        kernel,
        out_shape=jax.ShapeDtypeStruct(start_states.shape, f32),
        in_specs=[hbm] * 5,
        out_specs=vmem,
        scratch_shapes=[
            pltpu.VMEM((tracers, levels, rows, lat), f32),
            pltpu.VMEM((STEPS, tracers, levels + 2, rows, lat), f32),
            pltpu.VMEM((3, rows, lat), f32),
            pltpu.VMEM((levels, rows, lat), f32),
            pltpu.VMEM((3, nf + 2 * WIDE, lat), f32),
            pltpu.VMEM((2, tracers, levels, EDGE, lat), f32),
            pltpu.VMEM((2, levels, EDGE, lat), f32),
            packed, packed,
            pltpu.VMEM((9, levels, window, lanes), f32),
            coarse, coarse, shifts, edge, edge, edge, edge,
            shifts, edge, edge, edge, edge,
            pltpu.VMEM((nf, lat), jnp.int32),
            pltpu.SMEM(rates.shape, f32),
            pltpu.SemaphoreType.DMA((6,)),
            pltpu.SemaphoreType.DMA((copies,)),
            pltpu.SemaphoreType.DMA((copies,)),
        ],
        compiler_params=pltpu.CompilerParams(
            collective_id=0, has_side_effects=True, vmem_limit_bytes=64 * 1024 * 1024
        ),
    )(start_states, wet_levels, advection, forcing, rates)


def solution(mesh):
    return jax.shard_map(
        shards,
        mesh=mesh,
        in_specs=(
            P("tm", None, None, "space", None),
            P("space", None),
            P("space", None),
            P("space", None),
            P(),
        ),
        out_specs=P("tm", None, None, "space", None),
        check_vma=False,
    )
```

```python
import math

import jax
import jax.numpy as jnp
from jax import lax
from jax.experimental import pallas as pl
from jax.experimental.pallas import tpu as pltpu
from jax.sharding import PartitionSpec as P

STEPS = 4
SECTIONS = 4
COARSEN = 4
RELAX = 0.2
EDGE = 8
LANES = 128
CHUNK = 2
WIDE = COARSEN * SECTIONS
MESH = pl.DeviceIdType.MESH


def season_at(position, year):
    return 1.0 + 0.6 * jnp.sin(2.0 * math.pi * position / year)


def iota(shape, dim):
    return lax.broadcasted_iota(jnp.int32, shape, dim)


def dot(a, b):
    return jnp.dot(a, b, preferred_element_type=jnp.float32)


def split(value):
    parts = []
    for _ in range(3):
        part = value.astype(jnp.bfloat16)
        value = value - part.astype(jnp.float32)
        parts.append(part)
    return parts


def exact(flags, value):
    return jnp.where(flags, value, 0.0).astype(jnp.bfloat16)


def fold_rows(weights, value):
    if weights.shape[1] > value.shape[0]:
        rest = weights.shape[1] - value.shape[0]
        value = jnp.concatenate([value, jnp.zeros((rest, value.shape[1]), value.dtype)], 0)
    return dot(jnp.concatenate([weights] * 3, 1), jnp.concatenate(split(value), 0))


def kernel(
    start_ref, wet_hbm, flow_hbm, forcing_hbm, rates_hbm, out_ref,
    s_ref, state_ref, ring_ref, diag_ref, aux_ref, edge_ref, pack_ref, hr_ref, hl_ref,
    coef_ref, first_ref, jump_ref, x_ref, xl_ref, xr_ref, jl_ref, jr_ref,
    jn_ref, jnl_ref, jnr_ref, coarse_ref, o_ref, ol_ref, or_ref, pl_ref, pr_ref,
    wet_ref, rates_ref, local_sem, send_sem, recv_sem,
):
    _, tracers, levels, nf, lat = out_ref.shape
    nc = nf // COARSEN
    lc = lat // COARSEN
    lanes = 2 * lc
    window = coef_ref.shape[2]
    rows = nf + EDGE
    tm, n_tm = lax.axis_index("tm"), lax.axis_size("tm")
    space, n_space = lax.axis_index("space"), lax.axis_size("space")
    after, before = lax.rem(tm + 1, n_tm), lax.rem(tm + n_tm - 1, n_tm)
    later, earlier = lax.rem(tm + 2, n_tm), lax.rem(tm + n_tm - 2, n_tm)
    right, left = lax.rem(space + 1, n_space), lax.rem(space + n_space - 1, n_space)

    barrier = pltpu.get_barrier_semaphore()
    sources = [(tm, left), (tm, right)]
    sources += [(i, j) for i in (before, earlier) for j in (space, left, right)]
    for i, j in sources:
        pl.semaphore_signal(barrier, inc=1, device_id=(i, j), device_id_type=MESH)

    mid = pl.ds(WIDE, nf)
    loads = [
        pltpu.make_async_copy(src, dst, local_sem.at[i])
        for i, (src, dst) in enumerate((
            (wet_hbm, wet_ref),
            (flow_hbm, aux_ref.at[1, mid, :]),
            (forcing_hbm, aux_ref.at[2, mid, :]),
            (rates_hbm, rates_ref),
            (start_ref.at[0, :, :, pl.ds(0, EDGE), :], edge_ref.at[0]),
            (start_ref.at[0, :, :, pl.ds(nf - EDGE, EDGE), :], edge_ref.at[1]),
        ))
    ]
    for load in loads:
        load.start()
    where = jnp.minimum(iota((8, 128), 1).astype(jnp.float32) + 0.5, STEPS + 0.5)
    where = jnp.where(where > STEPS, STEPS * 0.5, where)
    begin = (before * STEPS).astype(jnp.float32)
    season_ref = season_at(begin + where, STEPS * n_tm)
    begin = (earlier * STEPS).astype(jnp.float32)
    season_before = season_at(begin + where, STEPS * n_tm)
    zero = jnp.zeros((tracers, rows, lat), jnp.float32)
    for step in range(STEPS):
        state_ref[step, :, 0] = zero
        state_ref[step, :, levels + 1] = zero
    for load in loads[:3]:
        load.wait()
    aux_ref[0, mid, :] = wet_ref[...].astype(jnp.float32)
    loads[4].wait()
    loads[5].wait()
    upper_half = iota((EDGE, lat), 0) < COARSEN
    for l in range(levels):
        pack_ref[0, l] = jnp.where(
            upper_half, edge_ref[0, 0, l], pltpu.roll(edge_ref[0, 1, l], COARSEN, 0)
        )
        pack_ref[1, l] = jnp.where(
            upper_half, pltpu.roll(edge_ref[1, 0, l], COARSEN, 0), edge_ref[1, 1, l]
        )
    pl.semaphore_wait(barrier, len(sources))

    def send(index, src, dst, i, j):
        copy = pltpu.make_async_remote_copy(
            src_ref=src, dst_ref=dst, send_sem=send_sem.at[index], recv_sem=recv_sem.at[index],
            device_id=(i, j), device_id_type=MESH,
        )
        copy.start()
        return copy

    sends = [
        send(0, aux_ref.at[:, pl.ds(nf, WIDE), :], aux_ref.at[:, pl.ds(0, WIDE), :], tm, right),
        send(1, aux_ref.at[:, pl.ds(WIDE, WIDE), :],
             aux_ref.at[:, pl.ds(WIDE + nf, WIDE), :], tm, left),
        send(2, pack_ref.at[0], hr_ref, after, left),
        send(3, pack_ref.at[1], hl_ref, after, right),
    ]

    def piece(index):
        part = pl.ds(index * CHUNK, CHUNK)
        return pltpu.make_async_remote_copy(
            src_ref=start_ref.at[0, :, part], dst_ref=s_ref.at[:, part, pl.ds(0, nf), :],
            send_sem=send_sem.at[13 + index], recv_sem=recv_sem.at[13 + index],
            device_id=(after, space), device_id_type=MESH,
        )

    pieces = levels // CHUNK
    for index in range(pieces):
        piece(index).start()

    loads[3].wait()
    sends[0].wait_recv()
    sends[1].wait_recv()
    half = iota((EDGE, lat), 0) < COARSEN
    for i in range(3):
        ring_ref[i, pl.ds(0, nf), :] = aux_ref[i, mid, :]
        ring_ref[i, pl.ds(nf, EDGE), :] = jnp.where(
            half, aux_ref[i, pl.ds(WIDE + nf, EDGE), :], aux_ref[i, pl.ds(WIDE - EDGE, EDGE), :]
        )
    wide = ring_ref[0]
    lane = iota((rows, lat), 1)
    wet_e = pltpu.roll(wide, rows - 1, 0)
    wet_w = pltpu.roll(wide, 1, 0)
    wet_n = jnp.where(lane == lat - 1, 0.0, pltpu.roll(wide, lat - 1, 1))
    wet_s = jnp.where(lane == 0, 0.0, pltpu.roll(wide, 1, 1))
    flow = ring_ref[1]
    for l in range(levels):
        k = rates_ref[0, l]
        west = jnp.where(wet_w > l, 1.0, 0.0)
        count = west
        for other in (wet_e, wet_n, wet_s):
            count = count + jnp.where(other > l, 1.0, 0.0)
        total = 1.0 - k * count - flow * west
        if l:
            total = total - rates_ref[1, l - 1]
        if l < levels - 1:
            total = total - jnp.where(wide > l + 1, rates_ref[1, l], 0.0)
        diag_ref[l] = total
    quarter = 1.0 / COARSEN
    group, folded = iota((lat, lanes), 0) // COARSEN, iota((lat, lanes), 1)
    fold0 = exact(group == folded, quarter)
    fold1 = exact(group + lc == folded, quarter)
    both = fold0 + fold1

    def gather_rows(count, base):
        shape = (window, count)
        return exact(iota(shape, 1) // COARSEN + base == iota(shape, 0), quarter)

    def fold_lat(nutrient, organic):
        pairs = zip(split(nutrient), split(organic))
        return sum(dot(first, fold0) + dot(second, fold1) for first, second in pairs)

    row = iota((window, lanes), 0)
    col = iota((window, lanes), 1)
    inner = (row >= SECTIONS) & (row < SECTIONS + nc)
    to_right = iota((8, lanes), 0) < SECTIONS
    tail = iota((8, lanes), 0) + (window - 8)
    to_left = (tail >= SECTIONS + nc) & (tail < 2 * SECTIONS + nc)

    wide_rows = gather_rows(nf + 2 * WIDE, 0)
    c_flow = fold_rows(wide_rows, fold_lat(aux_ref[1], aux_ref[1])) * (STEPS / COARSEN)
    c_forcing = fold_rows(wide_rows, fold_lat(aux_ref[2], aux_ref[2]))
    wet = aux_ref[0]
    masks = [
        dot(wide_rows, dot(exact(wet > l, 1.0), both).astype(jnp.bfloat16)) for l in range(levels)
    ]
    season = season_ref[0, STEPS]
    is_nutrient = col < lc
    edge_n = (col == lc - 1) | (col == lanes - 1)
    edge_s = (col == 0) | (col == lc)
    for l in range(levels):
        m = masks[l]
        k = rates_ref[0, l] * (STEPS / COARSEN**2)
        g = rates_ref[2, l] * STEPS * season
        g_before = rates_ref[2, l] * STEPS * season_before[0, STEPS]
        r = rates_ref[3, l] * STEPS
        q = RELAX * STEPS if l == 0 else 0.0
        m_w = pltpu.roll(m, 1, 0)
        east = k * pltpu.roll(m, window - 1, 0)
        west = (k + c_flow) * m_w
        north = k * jnp.where(edge_n, 0.0, pltpu.roll(m, lanes - 1, 1))
        south = k * jnp.where(edge_s, 0.0, pltpu.roll(m, 1, 1))
        total = 1.0 - east - west - north - south
        if l < levels - 1:
            down = rates_ref[1, l] * STEPS * masks[l + 1]
            total = total - down
            coef_ref[4, l] = down
        if l:
            up = rates_ref[1, l - 1] * STEPS * masks[l - 1]
            total = total - up
            coef_ref[5, l] = up
        coef_ref[0, l] = east
        coef_ref[1, l] = west
        coef_ref[2, l] = north
        coef_ref[3, l] = south
        coef_ref[6, l] = total
        coef_ref[7, l] = m * jnp.where(is_nutrient, 1.0 - g - q, 1.0 - r)
        coef_ref[8, l] = m * jnp.where(is_nutrient, r, g)
        coef_ref[9, l] = m * jnp.where(is_nutrient, 1.0 - g_before - q, 1.0 - r)
        coef_ref[10, l] = m * jnp.where(is_nutrient, r, g_before)
    surface = masks[0] * jnp.where(is_nutrient, RELAX * STEPS * c_forcing, 0.0)

    sends[2].wait_recv()
    sends[3].wait_recv()
    padded_rows = -(-rows // 16) * 16
    at, ring = iota((window, padded_rows), 0), iota((window, padded_rows), 1)
    start_rows = exact(
        ((ring < nf + COARSEN) & (ring // COARSEN + SECTIONS == at))
        | ((ring >= nf + COARSEN) & (ring < rows) & (at == SECTIONS - 1)),
        quarter,
    )

    def arrive(index):
        piece(index).wait_recv()
        part = pl.ds(index * CHUNK, CHUNK)
        for j in range(CHUNK):
            l = index * CHUNK + j
            high, low = hr_ref[l], hl_ref[l]
            s_ref[0, l, pl.ds(nf, EDGE), :] = jnp.where(half, high, pltpu.roll(low, COARSEN, 0))
            s_ref[1, l, pl.ds(nf, EDGE), :] = jnp.where(half, pltpu.roll(high, COARSEN, 0), low)
            here = ring_ref[0] > jnp.asarray(l, jnp.float32)
            for t in range(tracers):
                state_ref[0, t, l + 1] = jnp.where(here, s_ref[t, l], 0.0)
        flat = (CHUNK * rows, lat)
        folds = fold_lat(s_ref[0, part].reshape(flat), s_ref[1, part].reshape(flat))
        for j in range(CHUNK):
            value = fold_rows(start_rows, folds[j * rows:(j + 1) * rows])
            first_ref[index * CHUNK + j] = value

    sub = iota((EDGE, LANES), 0)
    lane = iota((EDGE, LANES), 1)
    blocks = rows // EDGE
    tiles = lat // LANES

    def fine_level(step, l):
        season = season_ref[0, step]
        k, v, g, r = (rates_ref[i, l] for i in range(4))
        upper = rates_ref[1, lax.rem(l + levels - 1, levels)]
        lf = l.astype(jnp.float32)
        grown = g * season
        q = jnp.where(l == 0, RELAX, 0.0)
        kept, stays = 1.0 - grown - q, 1.0 - r
        for x in range(tiles):
            across = pl.ds(x * LANES, LANES)
            cells, norths, souths = [], [], []
            for t in range(tracers):
                cell = [
                    state_ref[step, t, l + 1, pl.ds(b * EDGE, EDGE), across] for b in range(blocks)
                ]
                cells.append(
                    (cell, [pltpu.roll(c, EDGE - 1, 0) for c in cell],
                     [pltpu.roll(c, 1, 0) for c in cell])
                )
            for b in range(blocks if step < STEPS - 1 else blocks - 1):
                down_rows = pl.ds(b * EDGE, EDGE)
                centre = diag_ref[l, down_rows, across]
                speed = ring_ref[1, down_rows, across] + k
                here = ring_ref[0, down_rows, across] > lf
                mixed = []
                for t in range(tracers):
                    cell, fore, back = cells[t]
                    u = cell[b]
                    east = jnp.where(sub == EDGE - 1, fore[(b + 1) % blocks], fore[b])
                    west = jnp.where(sub == 0, back[(b + blocks - 1) % blocks], back[b])
                    if x + 1 < tiles:
                        ahead = state_ref[step, t, l + 1, down_rows, pl.ds((x + 1) * LANES, LANES)]
                        ahead = pltpu.roll(ahead, LANES - 1, 1)
                    else:
                        ahead = 0.0
                    if x:
                        behind = state_ref[step, t, l + 1, down_rows, pl.ds((x - 1) * LANES, LANES)]
                        behind = pltpu.roll(behind, 1, 1)
                    else:
                        behind = 0.0
                    north = jnp.where(lane == LANES - 1, ahead, pltpu.roll(u, LANES - 1, 1))
                    south = jnp.where(lane == 0, behind, pltpu.roll(u, 1, 1))
                    mixed.append(
                        centre * u + k * (east + north + south) + speed * west
                        + v * state_ref[step, t, l + 2, down_rows, across]
                        + upper * state_ref[step, t, l, down_rows, across]
                    )
                nutrient = mixed[0] * kept + r * mixed[1] + q * ring_ref[2, down_rows, across]
                organic = mixed[1] * stays + grown * mixed[0]
                nutrient = jnp.where(here, nutrient, 0.0)
                organic = jnp.where(here, organic, 0.0)
                if step < STEPS - 1:
                    state_ref[step + 1, 0, l + 1, down_rows, across] = nutrient
                    state_ref[step + 1, 1, l + 1, down_rows, across] = organic
                else:
                    out_ref[0, 0, l, down_rows, across] = nutrient
                    out_ref[0, 1, l, down_rows, across] = organic

    arrive(0)

    def diagonal(d, carry):
        @pl.when((lax.rem(d + 1, CHUNK) == 0) & (d + 1 < levels))
        def _():
            arrive((d + 1) // CHUNK)

        for step in range(STEPS):
            @pl.when((d >= step) & (d < levels + step))
            def _():
                fine_level(step, d - step)

        return carry

    lax.fori_loop(0, levels + STEPS - 1, diagonal, 0)

    def halo_parts(value):
        low = jnp.where(to_right, pltpu.roll(value, window - nc, 0)[:8], 0.0)
        high = jnp.where(to_left, pltpu.roll(value, nc, 0)[window - 8:], 0.0)
        return low, high

    full = -(-(nc + SECTIONS) // 8) * 8
    pairs = levels // 2

    def put_halos(values, low_ref, high_ref):
        parts = [halo_parts(value) for value in values]
        for l in range(pairs):
            for ref, first, second in zip((low_ref, high_ref), parts[l], parts[l + pairs]):
                ref[l] = first + pltpu.roll(second, SECTIONS, 0)

    def get_halo(ref, flags, l):
        value = ref[l % pairs]
        if l >= pairs:
            value = pltpu.roll(value, SECTIONS, 0)
        return jnp.where(flags, value, 0.0)

    def widened(value, low_ref, high_ref, l):
        low, high = get_halo(low_ref, to_right, l), get_halo(high_ref, to_left, l)
        pieces = [value[:8] + low, value[8:window - 8]]
        pieces.append(value[window - 8:] + high if full == window else high)
        return jnp.concatenate(pieces, 0)

    centre_rows = gather_rows(nf, SECTIONS)
    chunk = levels // SECTIONS
    flat = (chunk * nf, lat)
    ends = []
    for c in range(SECTIONS):
        part = pl.ds(c * chunk, chunk)
        folds = fold_lat(out_ref[0, 0, part].reshape(flat), out_ref[0, 1, part].reshape(flat))
        for j in range(chunk):
            l = c * chunk + j
            value = fold_rows(centre_rows, folds[j * nf:(j + 1) * nf])
            o_ref[0, l] = value
            ends.append(value)
    put_halos(ends, ol_ref, or_ref)
    filled = pl.ds(0, full)
    sends += [
        send(4, o_ref.at[0, :, filled], x_ref.at[0, :, filled], later, space),
        send(5, ol_ref, xl_ref, later, right),
        send(6, or_ref, xr_ref, later, left),
    ]

    def coarse_step(load_level, own=True):
        fields = [load_level(l) for l in range(levels)]
        results = []
        for l in range(levels):
            u = fields[l]
            w = coef_ref[6, l] * u
            w = w + coef_ref[0, l] * pltpu.roll(u, window - 1, 0)
            w = w + coef_ref[1, l] * pltpu.roll(u, 1, 0)
            w = w + coef_ref[2, l] * pltpu.roll(u, lanes - 1, 1)
            w = w + coef_ref[3, l] * pltpu.roll(u, 1, 1)
            if l < levels - 1:
                w = w + coef_ref[4, l] * fields[l + 1]
            if l:
                w = w + coef_ref[5, l] * fields[l - 1]
            kept, mixed = (7, 8) if own else (9, 10)
            value = coef_ref[kept, l] * w + coef_ref[mixed, l] * pltpu.roll(w, lc, 1)
            if l == 0:
                value = value + surface
            results.append(value)
        return results

    jumps = []
    for l, value in enumerate(coarse_step(lambda l: first_ref[l])):
        value = jnp.where(inner, value, 0.0)
        first_ref[l] = value
        jump = o_ref[0, l] - value
        jump_ref[l] = jump
        jumps.append(jump)
    put_halos(jumps, pl_ref, pr_ref)
    sends += [
        send(9, jump_ref.at[:, filled], jn_ref.at[:, filled], after, space),
        send(10, pl_ref, jnl_ref, after, right),
        send(11, pr_ref, jnr_ref, after, left),
        send(7, pl_ref, jl_ref, tm, right),
        send(8, pr_ref, jr_ref, tm, left),
    ]

    for copy in sends[4:7]:
        copy.wait_recv()
    results = coarse_step(lambda l: widened(x_ref[0, l], xl_ref, xr_ref, l), own=False)
    for copy in sends[7:10]:
        copy.wait_recv()
    for l in range(levels):
        jump = widened(jn_ref[l], jnl_ref, jnr_ref, l)
        coarse_ref[0, l] = jump
        coarse_ref[1, l] = results[l] + jump
    results = coarse_step(lambda l: coarse_ref[1, l])
    for copy in sends[10:12]:
        copy.wait_recv()
    narrow = full < window
    for l in range(levels):
        value = results[l] + widened(jump_ref[l], jl_ref, jr_ref, l)
        o_ref[1, l] = pltpu.roll(value, window - SECTIONS // 2, 0) if narrow else value
    sends.append(send(12, o_ref.at[1, :, filled], x_ref.at[1, :, filled], later, space))

    def arrived(l):
        value = x_ref[1, l]
        if narrow:
            value = jnp.concatenate([value[:full], jnp.zeros((window - full, lanes), value.dtype)], 0)
            value = pltpu.roll(value, SECTIONS // 2, 0)
        return value

    sends[12].wait_recv()
    results = coarse_step(arrived, own=False)
    for l in range(levels):
        coarse_ref[1, l] = results[l] + coarse_ref[0, l]
    results = coarse_step(lambda l: coarse_ref[1, l])

    shape = (nf, window)
    spread_rows = exact(iota(shape, 0) // COARSEN + SECTIONS == iota(shape, 1), 1.0)
    shape = (lanes, lat)
    group = iota(shape, 1) // COARSEN
    spread0 = exact(group == iota(shape, 0), 1.0)
    spread1 = exact(group + lc == iota(shape, 0), 1.0)
    for c in range(SECTIONS):
        stacked = []
        for l in range(c * chunk, (c + 1) * chunk):
            stacked.append([
                dot(spread_rows, part).astype(jnp.bfloat16) for part in split(results[l] - first_ref[l])
            ])
        parts = [jnp.concatenate(same, 0) for same in zip(*stacked)]
        for t, spread in enumerate((spread0, spread1)):
            value = sum(dot(part, spread) for part in parts).reshape(chunk, nf, lat)
            part = pl.ds(c * chunk, chunk)
            out_ref[0, t, part] = out_ref[0, t, part] + value
    for copy in sends:
        copy.wait_send()
    for index in range(pieces):
        piece(index).wait_send()


def shards(start_states, wet_levels, advection, forcing, rates):
    _, tracers, levels, nf, lat = start_states.shape
    nc = nf // COARSEN
    lanes = 2 * (lat // COARSEN)
    window = -(-(nc + 2 * SECTIONS) // 8) * 8
    rows = nf + EDGE
    f32 = jnp.float32
    packed = pltpu.VMEM((levels, EDGE, lat), f32)
    coarse = pltpu.VMEM((levels, window, lanes), f32)
    edge = pltpu.VMEM((levels // 2, 8, lanes), f32)
    shifts = pltpu.VMEM((2, levels, window, lanes), f32)
    copies = 13 + levels // CHUNK
    vmem = pl.BlockSpec(memory_space=pltpu.VMEM)
    hbm = pl.BlockSpec(memory_space=pltpu.HBM)
    return pl.pallas_call(
        kernel,
        out_shape=jax.ShapeDtypeStruct(start_states.shape, f32),
        in_specs=[hbm] * 5,
        out_specs=vmem,
        scratch_shapes=[
            pltpu.VMEM((tracers, levels, rows, lat), f32),
            pltpu.VMEM((STEPS, tracers, levels + 2, rows, lat), f32),
            pltpu.VMEM((3, rows, lat), f32),
            pltpu.VMEM((levels, rows, lat), f32),
            pltpu.VMEM((3, nf + 2 * WIDE, lat), f32),
            pltpu.VMEM((2, tracers, levels, EDGE, lat), f32),
            pltpu.VMEM((2, levels, EDGE, lat), f32),
            packed, packed,
            pltpu.VMEM((11, levels, window, lanes), f32),
            coarse, coarse, shifts, edge, edge, edge, edge,
            coarse, edge, edge, shifts, shifts, edge, edge, edge, edge,
            pltpu.VMEM((nf, lat), jnp.int32),
            pltpu.SMEM(rates.shape, f32),
            pltpu.SemaphoreType.DMA((6,)),
            pltpu.SemaphoreType.DMA((copies,)),
            pltpu.SemaphoreType.DMA((copies,)),
        ],
        compiler_params=pltpu.CompilerParams(
            collective_id=0, has_side_effects=True, vmem_limit_bytes=64 * 1024 * 1024
        ),
    )(start_states, wet_levels, advection, forcing, rates)


def solution(mesh):
    return jax.shard_map(
        shards,
        mesh=mesh,
        in_specs=(
            P("tm", None, None, "space", None),
            P("space", None),
            P("space", None),
            P("space", None),
            P(),
        ),
        out_specs=P("tm", None, None, "space", None),
        check_vma=False,
    )
```

```python
import math

import jax
import jax.numpy as jnp
from jax import lax
from jax.experimental import pallas as pl
from jax.experimental.pallas import tpu as pltpu
from jax.sharding import PartitionSpec as P

STEPS = 4
SECTIONS = 4
COARSEN = 4
RELAX = 0.2
EDGE = 8
LANES = 128
CHUNK = 2
WIDE = COARSEN * SECTIONS
MESH = pl.DeviceIdType.MESH


def season_at(position, year):
    return 1.0 + 0.6 * jnp.sin(2.0 * math.pi * position / year)


def iota(shape, dim):
    return lax.broadcasted_iota(jnp.int32, shape, dim)


def dot(a, b):
    return jnp.dot(a, b, preferred_element_type=jnp.float32)


def split(value):
    parts = []
    for _ in range(3):
        part = value.astype(jnp.bfloat16)
        value = value - part.astype(jnp.float32)
        parts.append(part)
    return parts


def exact(flags, value):
    return jnp.where(flags, value, 0.0).astype(jnp.bfloat16)


def fold_rows(weights, value):
    if weights.shape[1] > value.shape[0]:
        rest = weights.shape[1] - value.shape[0]
        value = jnp.concatenate([value, jnp.zeros((rest, value.shape[1]), value.dtype)], 0)
    return dot(jnp.concatenate([weights] * 3, 1), jnp.concatenate(split(value), 0))


def kernel(
    start_ref, wet_hbm, flow_hbm, forcing_hbm, rates_hbm, end_hbm, delta_ref,
    end_ref,    s_ref, state_ref, ring_ref, diag_ref, aux_ref, edge_ref, pack_ref, hr_ref, hl_ref,
    coef_ref, first_ref, jump_ref, x_ref, xl_ref, xr_ref, jl_ref, jr_ref,
    jn_ref, jnl_ref, jnr_ref, coarse_ref, o_ref, ol_ref, or_ref, pl_ref, pr_ref,
    wet_ref, rates_ref, local_sem, send_sem, recv_sem,
):
    tracers, levels, nf, lat = end_ref.shape
    nc = nf // COARSEN
    lc = lat // COARSEN
    lanes = 2 * lc
    window = coef_ref.shape[2]
    rows = nf + EDGE
    tm, n_tm = lax.axis_index("tm"), lax.axis_size("tm")
    space, n_space = lax.axis_index("space"), lax.axis_size("space")
    after, before = lax.rem(tm + 1, n_tm), lax.rem(tm + n_tm - 1, n_tm)
    later, earlier = lax.rem(tm + 2, n_tm), lax.rem(tm + n_tm - 2, n_tm)
    right, left = lax.rem(space + 1, n_space), lax.rem(space + n_space - 1, n_space)

    barrier = pltpu.get_barrier_semaphore()
    sources = [(tm, left), (tm, right)]
    sources += [(i, j) for i in (before, earlier) for j in (space, left, right)]
    for i, j in sources:
        pl.semaphore_signal(barrier, inc=1, device_id=(i, j), device_id_type=MESH)

    mid = pl.ds(WIDE, nf)
    loads = [
        pltpu.make_async_copy(src, dst, local_sem.at[i])
        for i, (src, dst) in enumerate((
            (wet_hbm, wet_ref),
            (flow_hbm, aux_ref.at[1, mid, :]),
            (forcing_hbm, aux_ref.at[2, mid, :]),
            (rates_hbm, rates_ref),
            (start_ref.at[0, :, :, pl.ds(0, EDGE), :], edge_ref.at[0]),
            (start_ref.at[0, :, :, pl.ds(nf - EDGE, EDGE), :], edge_ref.at[1]),
        ))
    ]
    for load in loads:
        load.start()
    where = jnp.minimum(iota((8, 128), 1).astype(jnp.float32) + 0.5, STEPS + 0.5)
    where = jnp.where(where > STEPS, STEPS * 0.5, where)
    begin = (before * STEPS).astype(jnp.float32)
    season_ref = season_at(begin + where, STEPS * n_tm)
    begin = (earlier * STEPS).astype(jnp.float32)
    season_before = season_at(begin + where, STEPS * n_tm)
    zero = jnp.zeros((tracers, rows, lat), jnp.float32)
    for step in range(STEPS):
        state_ref[step, :, 0] = zero
        state_ref[step, :, levels + 1] = zero
    for load in loads[:3]:
        load.wait()
    aux_ref[0, mid, :] = wet_ref[...].astype(jnp.float32)
    loads[4].wait()
    loads[5].wait()
    upper_half = iota((EDGE, lat), 0) < COARSEN
    for l in range(levels):
        pack_ref[0, l] = jnp.where(
            upper_half, edge_ref[0, 0, l], pltpu.roll(edge_ref[0, 1, l], COARSEN, 0)
        )
        pack_ref[1, l] = jnp.where(
            upper_half, pltpu.roll(edge_ref[1, 0, l], COARSEN, 0), edge_ref[1, 1, l]
        )
    pl.semaphore_wait(barrier, len(sources))

    def send(index, src, dst, i, j):
        copy = pltpu.make_async_remote_copy(
            src_ref=src, dst_ref=dst, send_sem=send_sem.at[index], recv_sem=recv_sem.at[index],
            device_id=(i, j), device_id_type=MESH,
        )
        copy.start()
        return copy

    sends = [
        send(0, aux_ref.at[:, pl.ds(nf, WIDE), :], aux_ref.at[:, pl.ds(0, WIDE), :], tm, right),
        send(1, aux_ref.at[:, pl.ds(WIDE, WIDE), :],
             aux_ref.at[:, pl.ds(WIDE + nf, WIDE), :], tm, left),
        send(2, pack_ref.at[0], hr_ref, after, left),
        send(3, pack_ref.at[1], hl_ref, after, right),
    ]

    def piece(index):
        part = pl.ds(index * CHUNK, CHUNK)
        return pltpu.make_async_remote_copy(
            src_ref=start_ref.at[0, :, part], dst_ref=s_ref.at[:, part, pl.ds(0, nf), :],
            send_sem=send_sem.at[13 + index], recv_sem=recv_sem.at[13 + index],
            device_id=(after, space), device_id_type=MESH,
        )

    pieces = levels // CHUNK
    for index in range(pieces):
        piece(index).start()

    loads[3].wait()
    sends[0].wait_recv()
    sends[1].wait_recv()
    half = iota((EDGE, lat), 0) < COARSEN
    for i in range(3):
        ring_ref[i, pl.ds(0, nf), :] = aux_ref[i, mid, :]
        ring_ref[i, pl.ds(nf, EDGE), :] = jnp.where(
            half, aux_ref[i, pl.ds(WIDE + nf, EDGE), :], aux_ref[i, pl.ds(WIDE - EDGE, EDGE), :]
        )
    wide = ring_ref[0]
    lane = iota((rows, lat), 1)
    wet_e = pltpu.roll(wide, rows - 1, 0)
    wet_w = pltpu.roll(wide, 1, 0)
    wet_n = jnp.where(lane == lat - 1, 0.0, pltpu.roll(wide, lat - 1, 1))
    wet_s = jnp.where(lane == 0, 0.0, pltpu.roll(wide, 1, 1))
    flow = ring_ref[1]
    for l in range(levels):
        k = rates_ref[0, l]
        west = jnp.where(wet_w > l, 1.0, 0.0)
        count = west
        for other in (wet_e, wet_n, wet_s):
            count = count + jnp.where(other > l, 1.0, 0.0)
        total = 1.0 - k * count - flow * west
        if l:
            total = total - rates_ref[1, l - 1]
        if l < levels - 1:
            total = total - jnp.where(wide > l + 1, rates_ref[1, l], 0.0)
        diag_ref[l] = total
    quarter = 1.0 / COARSEN
    group, folded = iota((lat, lanes), 0) // COARSEN, iota((lat, lanes), 1)
    fold0 = exact(group == folded, quarter)
    fold1 = exact(group + lc == folded, quarter)
    both = fold0 + fold1

    def gather_rows(count, base):
        shape = (window, count)
        return exact(iota(shape, 1) // COARSEN + base == iota(shape, 0), quarter)

    def fold_lat(nutrient, organic):
        pairs = zip(split(nutrient), split(organic))
        return sum(dot(first, fold0) + dot(second, fold1) for first, second in pairs)

    row = iota((window, lanes), 0)
    col = iota((window, lanes), 1)
    inner = (row >= SECTIONS) & (row < SECTIONS + nc)
    to_right = iota((8, lanes), 0) < SECTIONS
    tail = iota((8, lanes), 0) + (window - 8)
    to_left = (tail >= SECTIONS + nc) & (tail < 2 * SECTIONS + nc)

    wide_rows = gather_rows(nf + 2 * WIDE, 0)
    c_flow = fold_rows(wide_rows, fold_lat(aux_ref[1], aux_ref[1])) * (STEPS / COARSEN)
    c_forcing = fold_rows(wide_rows, fold_lat(aux_ref[2], aux_ref[2]))
    wet = aux_ref[0]
    masks = [
        dot(wide_rows, dot(exact(wet > l, 1.0), both).astype(jnp.bfloat16)) for l in range(levels)
    ]
    season = season_ref[0, STEPS]
    is_nutrient = col < lc
    edge_n = (col == lc - 1) | (col == lanes - 1)
    edge_s = (col == 0) | (col == lc)
    for l in range(levels):
        m = masks[l]
        k = rates_ref[0, l] * (STEPS / COARSEN**2)
        g = rates_ref[2, l] * STEPS * season
        g_before = rates_ref[2, l] * STEPS * season_before[0, STEPS]
        r = rates_ref[3, l] * STEPS
        q = RELAX * STEPS if l == 0 else 0.0
        m_w = pltpu.roll(m, 1, 0)
        east = k * pltpu.roll(m, window - 1, 0)
        west = (k + c_flow) * m_w
        north = k * jnp.where(edge_n, 0.0, pltpu.roll(m, lanes - 1, 1))
        south = k * jnp.where(edge_s, 0.0, pltpu.roll(m, 1, 1))
        total = 1.0 - east - west - north - south
        if l < levels - 1:
            down = rates_ref[1, l] * STEPS * masks[l + 1]
            total = total - down
            coef_ref[4, l] = down
        if l:
            up = rates_ref[1, l - 1] * STEPS * masks[l - 1]
            total = total - up
            coef_ref[5, l] = up
        coef_ref[0, l] = east
        coef_ref[1, l] = west
        coef_ref[2, l] = north
        coef_ref[3, l] = south
        coef_ref[6, l] = total
        coef_ref[7, l] = m * jnp.where(is_nutrient, 1.0 - g - q, 1.0 - r)
        coef_ref[8, l] = m * jnp.where(is_nutrient, r, g)
        coef_ref[9, l] = m * jnp.where(is_nutrient, 1.0 - g_before - q, 1.0 - r)
        coef_ref[10, l] = m * jnp.where(is_nutrient, r, g_before)
    surface = masks[0] * jnp.where(is_nutrient, RELAX * STEPS * c_forcing, 0.0)

    sends[2].wait_recv()
    sends[3].wait_recv()
    padded_rows = -(-rows // 16) * 16
    at, ring = iota((window, padded_rows), 0), iota((window, padded_rows), 1)
    start_rows = exact(
        ((ring < nf + COARSEN) & (ring // COARSEN + SECTIONS == at))
        | ((ring >= nf + COARSEN) & (ring < rows) & (at == SECTIONS - 1)),
        quarter,
    )

    centre_rows = gather_rows(nf, SECTIONS)

    def fold_end(first, count):
        part = pl.ds(first, count)
        flat = (count * nf, lat)
        folds = fold_lat(end_ref[0, part].reshape(flat), end_ref[1, part].reshape(flat))
        for j in range(count):
            o_ref[0, first + j] = fold_rows(centre_rows, folds[j * nf:(j + 1) * nf])

    def fold_start(index):
        part = pl.ds(index * CHUNK, CHUNK)
        flat = (CHUNK * rows, lat)
        folds = fold_lat(s_ref[0, part].reshape(flat), s_ref[1, part].reshape(flat))
        for j in range(CHUNK):
            value = fold_rows(start_rows, folds[j * rows:(j + 1) * rows])
            first_ref[index * CHUNK + j] = value

    def arrive(index):
        piece(index).wait_recv()
        for j in range(CHUNK):
            l = index * CHUNK + j
            high, low = hr_ref[l], hl_ref[l]
            s_ref[0, l, pl.ds(nf, EDGE), :] = jnp.where(half, high, pltpu.roll(low, COARSEN, 0))
            s_ref[1, l, pl.ds(nf, EDGE), :] = jnp.where(half, pltpu.roll(high, COARSEN, 0), low)
            here = ring_ref[0] > jnp.asarray(l, jnp.float32)
            for t in range(tracers):
                state_ref[0, t, l + 1] = jnp.where(here, s_ref[t, l], 0.0)

    sub = iota((EDGE, LANES), 0)
    lane = iota((EDGE, LANES), 1)
    blocks = rows // EDGE
    tiles = lat // LANES

    def fine_level(step, l):
        season = season_ref[0, step]
        k, v, g, r = (rates_ref[i, l] for i in range(4))
        upper = rates_ref[1, lax.rem(l + levels - 1, levels)]
        lf = l.astype(jnp.float32)
        grown = g * season
        q = jnp.where(l == 0, RELAX, 0.0)
        kept, stays = 1.0 - grown - q, 1.0 - r
        for x in range(tiles):
            across = pl.ds(x * LANES, LANES)
            cells, norths, souths = [], [], []
            for t in range(tracers):
                cell = [
                    state_ref[step, t, l + 1, pl.ds(b * EDGE, EDGE), across] for b in range(blocks)
                ]
                cells.append(
                    (cell, [pltpu.roll(c, EDGE - 1, 0) for c in cell],
                     [pltpu.roll(c, 1, 0) for c in cell])
                )
            for b in range(blocks if step < STEPS - 1 else blocks - 1):
                down_rows = pl.ds(b * EDGE, EDGE)
                centre = diag_ref[l, down_rows, across]
                speed = ring_ref[1, down_rows, across] + k
                here = ring_ref[0, down_rows, across] > lf
                mixed = []
                for t in range(tracers):
                    cell, fore, back = cells[t]
                    u = cell[b]
                    east = jnp.where(sub == EDGE - 1, fore[(b + 1) % blocks], fore[b])
                    west = jnp.where(sub == 0, back[(b + blocks - 1) % blocks], back[b])
                    if x + 1 < tiles:
                        ahead = state_ref[step, t, l + 1, down_rows, pl.ds((x + 1) * LANES, LANES)]
                        ahead = pltpu.roll(ahead, LANES - 1, 1)
                    else:
                        ahead = 0.0
                    if x:
                        behind = state_ref[step, t, l + 1, down_rows, pl.ds((x - 1) * LANES, LANES)]
                        behind = pltpu.roll(behind, 1, 1)
                    else:
                        behind = 0.0
                    north = jnp.where(lane == LANES - 1, ahead, pltpu.roll(u, LANES - 1, 1))
                    south = jnp.where(lane == 0, behind, pltpu.roll(u, 1, 1))
                    mixed.append(
                        centre * u + k * (east + north + south) + speed * west
                        + v * state_ref[step, t, l + 2, down_rows, across]
                        + upper * state_ref[step, t, l, down_rows, across]
                    )
                nutrient = mixed[0] * kept + r * mixed[1] + q * ring_ref[2, down_rows, across]
                organic = mixed[1] * stays + grown * mixed[0]
                nutrient = jnp.where(here, nutrient, 0.0)
                organic = jnp.where(here, organic, 0.0)
                if step < STEPS - 1:
                    state_ref[step + 1, 0, l + 1, down_rows, across] = nutrient
                    state_ref[step + 1, 1, l + 1, down_rows, across] = organic
                else:
                    end_ref[0, l, down_rows, across] = nutrient
                    end_ref[1, l, down_rows, across] = organic

    lag = 1 - (-STEPS // CHUNK)
    arrive(0)

    def diagonal(d, carry):
        @pl.when((lax.rem(d + 1, CHUNK) == 0) & (d + 1 < levels))
        def _():
            index = (d + 1) // CHUNK
            fold_start(index - 1)

            @pl.when(index >= lag)
            def _():
                fold_end((index - lag) * CHUNK, CHUNK)

            arrive(index)

        for step in range(STEPS):
            @pl.when((d >= step) & (d < levels + step))
            def _():
                fine_level(step, d - step)

        return carry

    lax.fori_loop(0, levels + STEPS - 1, diagonal, 0)

    def halo_parts(value):
        low = jnp.where(to_right, pltpu.roll(value, window - nc, 0)[:8], 0.0)
        high = jnp.where(to_left, pltpu.roll(value, nc, 0)[window - 8:], 0.0)
        return low, high

    full = -(-(nc + SECTIONS) // 8) * 8
    pairs = levels // 2

    def put_halos(values, low_ref, high_ref):
        parts = [halo_parts(value) for value in values]
        for l in range(pairs):
            for ref, first, second in zip((low_ref, high_ref), parts[l], parts[l + pairs]):
                ref[l] = first + pltpu.roll(second, SECTIONS, 0)

    def get_halo(ref, flags, l):
        value = ref[l % pairs]
        if l >= pairs:
            value = pltpu.roll(value, SECTIONS, 0)
        return jnp.where(flags, value, 0.0)

    def widened(value, low_ref, high_ref, l):
        low, high = get_halo(low_ref, to_right, l), get_halo(high_ref, to_left, l)
        pieces = [value[:8] + low, value[8:window - 8]]
        pieces.append(value[window - 8:] + high if full == window else high)
        return jnp.concatenate(pieces, 0)

    fold_end((pieces - lag) * CHUNK, lag * CHUNK)
    ends = [o_ref[0, l] for l in range(levels)]
    put_halos(ends, ol_ref, or_ref)
    filled = pl.ds(0, full)
    sends += [
        send(4, o_ref.at[0, :, filled], x_ref.at[0, :, filled], later, space),
        send(5, ol_ref, xl_ref, later, right),
        send(6, or_ref, xr_ref, later, left),
    ]

    def coarse_step(load_level, own=True):
        fields = [load_level(l) for l in range(levels)]
        results = []
        for l in range(levels):
            u = fields[l]
            w = coef_ref[6, l] * u
            w = w + coef_ref[0, l] * pltpu.roll(u, window - 1, 0)
            w = w + coef_ref[1, l] * pltpu.roll(u, 1, 0)
            w = w + coef_ref[2, l] * pltpu.roll(u, lanes - 1, 1)
            w = w + coef_ref[3, l] * pltpu.roll(u, 1, 1)
            if l < levels - 1:
                w = w + coef_ref[4, l] * fields[l + 1]
            if l:
                w = w + coef_ref[5, l] * fields[l - 1]
            kept, mixed = (7, 8) if own else (9, 10)
            value = coef_ref[kept, l] * w + coef_ref[mixed, l] * pltpu.roll(w, lc, 1)
            if l == 0:
                value = value + surface
            results.append(value)
        return results

    store = pltpu.make_async_copy(end_ref, end_hbm, local_sem.at[6])
    store.start()
    fold_start(pieces - 1)
    jumps = []
    for l, value in enumerate(coarse_step(lambda l: first_ref[l])):
        value = jnp.where(inner, value, 0.0)
        first_ref[l] = value
        jump = o_ref[0, l] - value
        jump_ref[l] = jump
        jumps.append(jump)
    put_halos(jumps, pl_ref, pr_ref)
    sends += [
        send(9, jump_ref.at[:, filled], jn_ref.at[:, filled], after, space),
        send(10, pl_ref, jnl_ref, after, right),
        send(11, pr_ref, jnr_ref, after, left),
        send(7, pl_ref, jl_ref, tm, right),
        send(8, pr_ref, jr_ref, tm, left),
    ]

    for copy in sends[4:7]:
        copy.wait_recv()
    results = coarse_step(lambda l: widened(x_ref[0, l], xl_ref, xr_ref, l), own=False)
    for copy in sends[7:10]:
        copy.wait_recv()
    for l in range(levels):
        jump = widened(jn_ref[l], jnl_ref, jnr_ref, l)
        coarse_ref[0, l] = jump
        coarse_ref[1, l] = results[l] + jump
    results = coarse_step(lambda l: coarse_ref[1, l])
    for copy in sends[10:12]:
        copy.wait_recv()
    narrow = full < window
    for l in range(levels):
        value = results[l] + widened(jump_ref[l], jl_ref, jr_ref, l)
        o_ref[1, l] = pltpu.roll(value, window - SECTIONS // 2, 0) if narrow else value
    sends.append(send(12, o_ref.at[1, :, filled], x_ref.at[1, :, filled], later, space))

    def arrived(l):
        value = x_ref[1, l]
        if narrow:
            value = jnp.concatenate([value[:full], jnp.zeros((window - full, lanes), value.dtype)], 0)
            value = pltpu.roll(value, SECTIONS // 2, 0)
        return value

    sends[12].wait_recv()
    results = coarse_step(arrived, own=False)
    for l in range(levels):
        coarse_ref[1, l] = results[l] + coarse_ref[0, l]
    results = coarse_step(lambda l: coarse_ref[1, l])

    for l in range(levels):
        delta_ref[l] = results[l] - first_ref[l]
    store.wait()
    for copy in sends:
        copy.wait_send()
    for index in range(pieces):
        piece(index).wait_send()


def finish(end_ref, delta_ref, out_ref):
    _, chunk, nf, lat = end_ref.shape
    _, window, lanes = delta_ref.shape
    lc = lanes // 2
    shape = (nf, window)
    spread_rows = exact(iota(shape, 0) // COARSEN + SECTIONS == iota(shape, 1), 1.0)
    shape = (lanes, lat)
    group = iota(shape, 1) // COARSEN
    spread0 = exact(group == iota(shape, 0), 1.0)
    spread1 = exact(group + lc == iota(shape, 0), 1.0)
    stacked = []
    for l in range(chunk):
        stacked.append([
            dot(spread_rows, part).astype(jnp.bfloat16) for part in split(delta_ref[l])
        ])
    parts = [jnp.concatenate(same, 0) for same in zip(*stacked)]
    for t, spread in enumerate((spread0, spread1)):
        value = sum(dot(part, spread) for part in parts).reshape(chunk, nf, lat)
        out_ref[0, t] = end_ref[t] + value


def shards(start_states, wet_levels, advection, forcing, rates):
    _, tracers, levels, nf, lat = start_states.shape
    nc = nf // COARSEN
    lanes = 2 * (lat // COARSEN)
    window = -(-(nc + 2 * SECTIONS) // 8) * 8
    rows = nf + EDGE
    f32 = jnp.float32
    packed = pltpu.VMEM((levels, EDGE, lat), f32)
    coarse = pltpu.VMEM((levels, window, lanes), f32)
    edge = pltpu.VMEM((levels // 2, 8, lanes), f32)
    shifts = pltpu.VMEM((2, levels, window, lanes), f32)
    copies = 13 + levels // CHUNK
    vmem = pl.BlockSpec(memory_space=pltpu.VMEM)
    hbm = pl.BlockSpec(memory_space=pltpu.HBM)
    ended, delta = pl.pallas_call(
        kernel,
        out_shape=[
            jax.ShapeDtypeStruct((tracers, levels, nf, lat), f32),
            jax.ShapeDtypeStruct((levels, window, lanes), f32),
        ],
        in_specs=[hbm] * 5,
        out_specs=[hbm, vmem],
        scratch_shapes=[
            pltpu.VMEM((tracers, levels, nf, lat), f32),
            pltpu.VMEM((tracers, levels, rows, lat), f32),
            pltpu.VMEM((STEPS, tracers, levels + 2, rows, lat), f32),
            pltpu.VMEM((3, rows, lat), f32),
            pltpu.VMEM((levels, rows, lat), f32),
            pltpu.VMEM((3, nf + 2 * WIDE, lat), f32),
            pltpu.VMEM((2, tracers, levels, EDGE, lat), f32),
            pltpu.VMEM((2, levels, EDGE, lat), f32),
            packed, packed,
            pltpu.VMEM((11, levels, window, lanes), f32),
            coarse, coarse, shifts, edge, edge, edge, edge,
            coarse, edge, edge, shifts, shifts, edge, edge, edge, edge,
            pltpu.VMEM((nf, lat), jnp.int32),
            pltpu.SMEM(rates.shape, f32),
            pltpu.SemaphoreType.DMA((7,)),
            pltpu.SemaphoreType.DMA((copies,)),
            pltpu.SemaphoreType.DMA((copies,)),
        ],
        compiler_params=pltpu.CompilerParams(
            collective_id=0, has_side_effects=True, vmem_limit_bytes=64 * 1024 * 1024
        ),
    )(start_states, wet_levels, advection, forcing, rates)
    chunk = levels // SECTIONS
    return pl.pallas_call(
        finish,
        grid=(SECTIONS,),
        out_shape=jax.ShapeDtypeStruct(start_states.shape, f32),
        in_specs=[
            pl.BlockSpec((tracers, chunk, nf, lat), lambda c: (0, c, 0, 0)),
            pl.BlockSpec((chunk, window, lanes), lambda c: (c, 0, 0)),
        ],
        out_specs=pl.BlockSpec((1, tracers, chunk, nf, lat), lambda c: (0, 0, c, 0, 0)),
        compiler_params=pltpu.CompilerParams(vmem_limit_bytes=64 * 1024 * 1024),
    )(ended, delta)


def solution(mesh):
    return jax.shard_map(
        shards,
        mesh=mesh,
        in_specs=(
            P("tm", None, None, "space", None),
            P("space", None),
            P("space", None),
            P("space", None),
            P(),
        ),
        out_specs=P("tm", None, None, "space", None),
        check_vma=False,
    )
```

```python
import math

import jax
import jax.numpy as jnp
from jax import lax
from jax.experimental import pallas as pl
from jax.experimental.pallas import tpu as pltpu
from jax.sharding import PartitionSpec as P

STEPS = 4
SECTIONS = 4
COARSEN = 4
RELAX = 0.2
EDGE = 8
LANES = 128
CHUNK = 2
WIDE = COARSEN * SECTIONS
MESH = pl.DeviceIdType.MESH


def season_at(position, year):
    return 1.0 + 0.6 * jnp.sin(2.0 * math.pi * position / year)


def iota(shape, dim):
    return lax.broadcasted_iota(jnp.int32, shape, dim)


def dot(a, b):
    return jnp.dot(a, b, preferred_element_type=jnp.float32)


def split(value):
    parts = []
    for _ in range(3):
        part = value.astype(jnp.bfloat16)
        value = value - part.astype(jnp.float32)
        parts.append(part)
    return parts


def exact(flags, value):
    return jnp.where(flags, value, 0.0).astype(jnp.bfloat16)


def fold_rows(weights, value):
    if weights.shape[1] > value.shape[0]:
        rest = weights.shape[1] - value.shape[0]
        value = jnp.concatenate([value, jnp.zeros((rest, value.shape[1]), value.dtype)], 0)
    return dot(jnp.concatenate([weights] * 3, 1), jnp.concatenate(split(value), 0))


def kernel(
    start_ref, wet_hbm, flow_hbm, forcing_hbm, rates_hbm, out_ref,
    s_ref, state_ref, ring_ref, diag_ref, aux_ref, edge_ref, pack_ref, hr_ref, hl_ref,
    coef_ref, first_ref, jump_ref, x_ref, xl_ref, xr_ref, jl_ref, jr_ref,
    jn_ref, jnl_ref, jnr_ref, coarse_ref, o_ref, ol_ref, or_ref, pl_ref, pr_ref,
    wet_ref, rates_ref, local_sem, send_sem, recv_sem,
):
    _, tracers, levels, nf, lat = out_ref.shape
    nc = nf // COARSEN
    lc = lat // COARSEN
    lanes = 2 * lc
    window = coef_ref.shape[2]
    rows = nf + EDGE
    tm, n_tm = lax.axis_index("tm"), lax.axis_size("tm")
    space, n_space = lax.axis_index("space"), lax.axis_size("space")
    after, before = lax.rem(tm + 1, n_tm), lax.rem(tm + n_tm - 1, n_tm)
    later, earlier = lax.rem(tm + 2, n_tm), lax.rem(tm + n_tm - 2, n_tm)
    right, left = lax.rem(space + 1, n_space), lax.rem(space + n_space - 1, n_space)

    barrier = pltpu.get_barrier_semaphore()
    sources = [(tm, left), (tm, right)]
    sources += [(i, j) for i in (before, earlier) for j in (space, left, right)]
    for i, j in sources:
        pl.semaphore_signal(barrier, inc=1, device_id=(i, j), device_id_type=MESH)

    mid = pl.ds(WIDE, nf)
    loads = [
        pltpu.make_async_copy(src, dst, local_sem.at[i])
        for i, (src, dst) in enumerate((
            (wet_hbm, wet_ref),
            (flow_hbm, aux_ref.at[1, mid, :]),
            (forcing_hbm, aux_ref.at[2, mid, :]),
            (rates_hbm, rates_ref),
            (start_ref.at[0, :, :, pl.ds(0, EDGE), :], edge_ref.at[0]),
            (start_ref.at[0, :, :, pl.ds(nf - EDGE, EDGE), :], edge_ref.at[1]),
        ))
    ]
    for load in loads:
        load.start()
    where = jnp.minimum(iota((8, 128), 1).astype(jnp.float32) + 0.5, STEPS + 0.5)
    where = jnp.where(where > STEPS, STEPS * 0.5, where)
    begin = (before * STEPS).astype(jnp.float32)
    season_ref = season_at(begin + where, STEPS * n_tm)
    begin = (earlier * STEPS).astype(jnp.float32)
    season_before = season_at(begin + where, STEPS * n_tm)
    zero = jnp.zeros((tracers, rows, lat), jnp.float32)
    for step in range(STEPS):
        state_ref[step, :, 0] = zero
        state_ref[step, :, levels + 1] = zero
    for load in loads[:3]:
        load.wait()
    aux_ref[0, mid, :] = wet_ref[...].astype(jnp.float32)
    loads[4].wait()
    loads[5].wait()
    upper_half = iota((EDGE, lat), 0) < COARSEN
    for l in range(levels):
        pack_ref[0, l] = jnp.where(
            upper_half, edge_ref[0, 0, l], pltpu.roll(edge_ref[0, 1, l], COARSEN, 0)
        )
        pack_ref[1, l] = jnp.where(
            upper_half, pltpu.roll(edge_ref[1, 0, l], COARSEN, 0), edge_ref[1, 1, l]
        )
    pl.semaphore_wait(barrier, len(sources))

    def send(index, src, dst, i, j):
        copy = pltpu.make_async_remote_copy(
            src_ref=src, dst_ref=dst, send_sem=send_sem.at[index], recv_sem=recv_sem.at[index],
            device_id=(i, j), device_id_type=MESH,
        )
        copy.start()
        return copy

    sends = [
        send(0, aux_ref.at[:, pl.ds(nf, WIDE), :], aux_ref.at[:, pl.ds(0, WIDE), :], tm, right),
        send(1, aux_ref.at[:, pl.ds(WIDE, WIDE), :],
             aux_ref.at[:, pl.ds(WIDE + nf, WIDE), :], tm, left),
        send(2, pack_ref.at[0], hr_ref, after, left),
        send(3, pack_ref.at[1], hl_ref, after, right),
    ]

    def piece(index):
        part = pl.ds(index * CHUNK, CHUNK)
        return pltpu.make_async_remote_copy(
            src_ref=start_ref.at[0, :, part], dst_ref=s_ref.at[:, part, pl.ds(0, nf), :],
            send_sem=send_sem.at[16 + index], recv_sem=recv_sem.at[16 + index],
            device_id=(after, space), device_id_type=MESH,
        )

    pieces = levels // CHUNK
    for index in range(pieces):
        piece(index).start()

    loads[3].wait()
    sends[0].wait_recv()
    sends[1].wait_recv()
    half = iota((EDGE, lat), 0) < COARSEN
    for i in range(3):
        ring_ref[i, pl.ds(0, nf), :] = aux_ref[i, mid, :]
        ring_ref[i, pl.ds(nf, EDGE), :] = jnp.where(
            half, aux_ref[i, pl.ds(WIDE + nf, EDGE), :], aux_ref[i, pl.ds(WIDE - EDGE, EDGE), :]
        )
    wide = ring_ref[0]
    lane = iota((rows, lat), 1)
    wet_e = pltpu.roll(wide, rows - 1, 0)
    wet_w = pltpu.roll(wide, 1, 0)
    wet_n = jnp.where(lane == lat - 1, 0.0, pltpu.roll(wide, lat - 1, 1))
    wet_s = jnp.where(lane == 0, 0.0, pltpu.roll(wide, 1, 1))
    flow = ring_ref[1]
    for l in range(levels):
        k = rates_ref[0, l]
        west = jnp.where(wet_w > l, 1.0, 0.0)
        count = west
        for other in (wet_e, wet_n, wet_s):
            count = count + jnp.where(other > l, 1.0, 0.0)
        total = 1.0 - k * count - flow * west
        if l:
            total = total - rates_ref[1, l - 1]
        if l < levels - 1:
            total = total - jnp.where(wide > l + 1, rates_ref[1, l], 0.0)
        diag_ref[l] = total
    quarter = 1.0 / COARSEN
    group, folded = iota((lat, lanes), 0) // COARSEN, iota((lat, lanes), 1)
    fold0 = exact(group == folded, quarter)
    fold1 = exact(group + lc == folded, quarter)
    both = fold0 + fold1

    def gather_rows(count, base):
        shape = (window, count)
        return exact(iota(shape, 1) // COARSEN + base == iota(shape, 0), quarter)

    def fold_lat(nutrient, organic):
        pairs = zip(split(nutrient), split(organic))
        return sum(dot(first, fold0) + dot(second, fold1) for first, second in pairs)

    row = iota((window, lanes), 0)
    col = iota((window, lanes), 1)
    inner = (row >= SECTIONS) & (row < SECTIONS + nc)
    to_right = iota((8, lanes), 0) < SECTIONS
    tail = iota((8, lanes), 0) + (window - 8)
    to_left = (tail >= SECTIONS + nc) & (tail < 2 * SECTIONS + nc)

    wide_rows = gather_rows(nf + 2 * WIDE, 0)
    c_flow = fold_rows(wide_rows, fold_lat(aux_ref[1], aux_ref[1])) * (STEPS / COARSEN)
    c_forcing = fold_rows(wide_rows, fold_lat(aux_ref[2], aux_ref[2]))
    wet = aux_ref[0]
    masks = [
        dot(wide_rows, dot(exact(wet > l, 1.0), both).astype(jnp.bfloat16)) for l in range(levels)
    ]
    season = season_ref[0, STEPS]
    is_nutrient = col < lc
    edge_n = (col == lc - 1) | (col == lanes - 1)
    edge_s = (col == 0) | (col == lc)
    for l in range(levels):
        m = masks[l]
        k = rates_ref[0, l] * (STEPS / COARSEN**2)
        g = rates_ref[2, l] * STEPS * season
        g_before = rates_ref[2, l] * STEPS * season_before[0, STEPS]
        r = rates_ref[3, l] * STEPS
        q = RELAX * STEPS if l == 0 else 0.0
        m_w = pltpu.roll(m, 1, 0)
        east = k * pltpu.roll(m, window - 1, 0)
        west = (k + c_flow) * m_w
        north = k * jnp.where(edge_n, 0.0, pltpu.roll(m, lanes - 1, 1))
        south = k * jnp.where(edge_s, 0.0, pltpu.roll(m, 1, 1))
        total = 1.0 - east - west - north - south
        if l < levels - 1:
            down = rates_ref[1, l] * STEPS * masks[l + 1]
            total = total - down
            coef_ref[4, l] = down
        if l:
            up = rates_ref[1, l - 1] * STEPS * masks[l - 1]
            total = total - up
            coef_ref[5, l] = up
        coef_ref[0, l] = east
        coef_ref[1, l] = west
        coef_ref[2, l] = north
        coef_ref[3, l] = south
        coef_ref[6, l] = total
        coef_ref[7, l] = m * jnp.where(is_nutrient, 1.0 - g - q, 1.0 - r)
        coef_ref[8, l] = m * jnp.where(is_nutrient, r, g)
        coef_ref[9, l] = m * jnp.where(is_nutrient, 1.0 - g_before - q, 1.0 - r)
        coef_ref[10, l] = m * jnp.where(is_nutrient, r, g_before)
    surface = masks[0] * jnp.where(is_nutrient, RELAX * STEPS * c_forcing, 0.0)

    sends[2].wait_recv()
    sends[3].wait_recv()
    padded_rows = -(-rows // 16) * 16
    at, ring = iota((window, padded_rows), 0), iota((window, padded_rows), 1)
    start_rows = exact(
        ((ring < nf + COARSEN) & (ring // COARSEN + SECTIONS == at))
        | ((ring >= nf + COARSEN) & (ring < rows) & (at == SECTIONS - 1)),
        quarter,
    )

    centre_rows = gather_rows(nf, SECTIONS)

    def halo_parts(value):
        low = jnp.where(to_right, pltpu.roll(value, window - nc, 0)[:8], 0.0)
        high = jnp.where(to_left, pltpu.roll(value, nc, 0)[window - 8:], 0.0)
        return low, high

    full = -(-(nc + SECTIONS) // 8) * 8

    def put_halos(values, low_ref, high_ref, first=0):
        parts = [halo_parts(value) for value in values]
        for l in range(len(parts) // 2):
            for ref, one, two in zip((low_ref, high_ref), parts[2 * l], parts[2 * l + 1]):
                ref[first + l] = one + pltpu.roll(two, SECTIONS, 0)

    def get_halo(ref, flags, l):
        value = ref[l // 2]
        if l % 2:
            value = pltpu.roll(value, SECTIONS, 0)
        return jnp.where(flags, value, 0.0)

    def widened(value, low_ref, high_ref, l):
        low, high = get_halo(low_ref, to_right, l), get_halo(high_ref, to_left, l)
        pieces = [value[:8] + low, value[8:window - 8]]
        pieces.append(value[window - 8:] + high if full == window else high)
        return jnp.concatenate(pieces, 0)

    def fold_end(first, count):
        part = pl.ds(first, count)
        flat = (count * nf, lat)
        folds = fold_lat(out_ref[0, 0, part].reshape(flat), out_ref[0, 1, part].reshape(flat))
        for j in range(count):
            o_ref[0, first + j] = fold_rows(centre_rows, folds[j * nf:(j + 1) * nf])

    def fold_start(index):
        part = pl.ds(index * CHUNK, CHUNK)
        flat = (CHUNK * rows, lat)
        folds = fold_lat(s_ref[0, part].reshape(flat), s_ref[1, part].reshape(flat))
        for j in range(CHUNK):
            value = fold_rows(start_rows, folds[j * rows:(j + 1) * rows])
            first_ref[index * CHUNK + j] = value

    def arrive(index):
        piece(index).wait_recv()
        for j in range(CHUNK):
            l = index * CHUNK + j
            high, low = hr_ref[l], hl_ref[l]
            s_ref[0, l, pl.ds(nf, EDGE), :] = jnp.where(half, high, pltpu.roll(low, COARSEN, 0))
            s_ref[1, l, pl.ds(nf, EDGE), :] = jnp.where(half, pltpu.roll(high, COARSEN, 0), low)
            here = ring_ref[0] > jnp.asarray(l, jnp.float32)
            for t in range(tracers):
                state_ref[0, t, l + 1] = jnp.where(here, s_ref[t, l], 0.0)

    sub = iota((EDGE, LANES), 0)
    lane = iota((EDGE, LANES), 1)
    blocks = rows // EDGE
    tiles = lat // LANES

    def fine_level(step, l):
        season = season_ref[0, step]
        k, v, g, r = (rates_ref[i, l] for i in range(4))
        upper = rates_ref[1, lax.rem(l + levels - 1, levels)]
        lf = l.astype(jnp.float32)
        grown = g * season
        q = jnp.where(l == 0, RELAX, 0.0)
        kept, stays = 1.0 - grown - q, 1.0 - r
        for x in range(tiles):
            across = pl.ds(x * LANES, LANES)
            cells, norths, souths = [], [], []
            for t in range(tracers):
                cell = [
                    state_ref[step, t, l + 1, pl.ds(b * EDGE, EDGE), across] for b in range(blocks)
                ]
                cells.append(
                    (cell, [pltpu.roll(c, EDGE - 1, 0) for c in cell],
                     [pltpu.roll(c, 1, 0) for c in cell])
                )
            for b in range(blocks if step < STEPS - 1 else blocks - 1):
                down_rows = pl.ds(b * EDGE, EDGE)
                centre = diag_ref[l, down_rows, across]
                speed = ring_ref[1, down_rows, across] + k
                here = ring_ref[0, down_rows, across] > lf
                mixed = []
                for t in range(tracers):
                    cell, fore, back = cells[t]
                    u = cell[b]
                    east = jnp.where(sub == EDGE - 1, fore[(b + 1) % blocks], fore[b])
                    west = jnp.where(sub == 0, back[(b + blocks - 1) % blocks], back[b])
                    if x + 1 < tiles:
                        ahead = state_ref[step, t, l + 1, down_rows, pl.ds((x + 1) * LANES, LANES)]
                        ahead = pltpu.roll(ahead, LANES - 1, 1)
                    else:
                        ahead = 0.0
                    if x:
                        behind = state_ref[step, t, l + 1, down_rows, pl.ds((x - 1) * LANES, LANES)]
                        behind = pltpu.roll(behind, 1, 1)
                    else:
                        behind = 0.0
                    north = jnp.where(lane == LANES - 1, ahead, pltpu.roll(u, LANES - 1, 1))
                    south = jnp.where(lane == 0, behind, pltpu.roll(u, 1, 1))
                    mixed.append(
                        centre * u + k * (east + north + south) + speed * west
                        + v * state_ref[step, t, l + 2, down_rows, across]
                        + upper * state_ref[step, t, l, down_rows, across]
                    )
                nutrient = mixed[0] * kept + r * mixed[1] + q * ring_ref[2, down_rows, across]
                organic = mixed[1] * stays + grown * mixed[0]
                nutrient = jnp.where(here, nutrient, 0.0)
                organic = jnp.where(here, organic, 0.0)
                if step < STEPS - 1:
                    state_ref[step + 1, 0, l + 1, down_rows, across] = nutrient
                    state_ref[step + 1, 1, l + 1, down_rows, across] = organic
                else:
                    out_ref[0, 0, l, down_rows, across] = nutrient
                    out_ref[0, 1, l, down_rows, across] = organic

    lag = 1 - (-STEPS // CHUNK)
    early = (pieces - lag) * CHUNK
    filled = pl.ds(0, full)

    def ends(first, count, index):
        part, pairs = pl.ds(first, count), pl.ds(first // 2, count // 2)
        routes = (
            (o_ref.at[0, part, filled], x_ref.at[0, part, filled], space),
            (ol_ref.at[pairs], xl_ref.at[pairs], right),
            (or_ref.at[pairs], xr_ref.at[pairs], left),
        )
        return [
            pltpu.make_async_remote_copy(
                src_ref=src, dst_ref=dst, send_sem=send_sem.at[index + i],
                recv_sem=recv_sem.at[index + i], device_id=(later, j), device_id_type=MESH,
            )
            for i, (src, dst, j) in enumerate(routes)
        ]

    arrive(0)

    def diagonal(d, carry):
        @pl.when((lax.rem(d + 1, CHUNK) == 0) & (d + 1 < levels))
        def _():
            index = (d + 1) // CHUNK
            fold_start(index - 1)

            @pl.when(index >= lag)
            def _():
                fold_end((index - lag) * CHUNK, CHUNK)

            arrive(index)

            @pl.when(index == pieces - 1)
            def _():
                put_halos([o_ref[0, l] for l in range(early)], ol_ref, or_ref)
                for copy in ends(0, early, 13):
                    copy.start()

        for step in range(STEPS):
            @pl.when((d >= step) & (d < levels + step))
            def _():
                fine_level(step, d - step)

        return carry

    lax.fori_loop(0, levels + STEPS - 1, diagonal, 0)

    fold_end((pieces - lag) * CHUNK, lag * CHUNK)
    put_halos([o_ref[0, l] for l in range(early, levels)], ol_ref, or_ref, early // 2)
    sends += [copy for copy in ends(0, early, 13)]
    for copy in ends(early, levels - early, 4):
        copy.start()
        sends.append(copy)

    def coarse_step(load_level, own=True):
        fields = [load_level(l) for l in range(levels)]
        results = []
        for l in range(levels):
            u = fields[l]
            w = coef_ref[6, l] * u
            w = w + coef_ref[0, l] * pltpu.roll(u, window - 1, 0)
            w = w + coef_ref[1, l] * pltpu.roll(u, 1, 0)
            w = w + coef_ref[2, l] * pltpu.roll(u, lanes - 1, 1)
            w = w + coef_ref[3, l] * pltpu.roll(u, 1, 1)
            if l < levels - 1:
                w = w + coef_ref[4, l] * fields[l + 1]
            if l:
                w = w + coef_ref[5, l] * fields[l - 1]
            kept, mixed = (7, 8) if own else (9, 10)
            value = coef_ref[kept, l] * w + coef_ref[mixed, l] * pltpu.roll(w, lc, 1)
            if l == 0:
                value = value + surface
            results.append(value)
        return results

    fold_start(pieces - 1)
    jumps = []
    for l, value in enumerate(coarse_step(lambda l: first_ref[l])):
        value = jnp.where(inner, value, 0.0)
        first_ref[l] = value
        jump = o_ref[0, l] - value
        jump_ref[l] = jump
        jumps.append(jump)
    put_halos(jumps, pl_ref, pr_ref)
    sends += [
        send(9, jump_ref.at[:, filled], jn_ref.at[:, filled], after, space),
        send(10, pl_ref, jnl_ref, after, right),
        send(11, pr_ref, jnr_ref, after, left),
        send(7, pl_ref, jl_ref, tm, right),
        send(8, pr_ref, jr_ref, tm, left),
    ]

    for copy in sends[4:10]:
        copy.wait_recv()
    results = coarse_step(lambda l: widened(x_ref[0, l], xl_ref, xr_ref, l), own=False)
    for copy in sends[10:13]:
        copy.wait_recv()
    for l in range(levels):
        jump = widened(jn_ref[l], jnl_ref, jnr_ref, l)
        coarse_ref[0, l] = jump
        coarse_ref[1, l] = results[l] + jump
    results = coarse_step(lambda l: coarse_ref[1, l])
    for copy in sends[13:15]:
        copy.wait_recv()
    narrow = full < window
    for l in range(levels):
        value = results[l] + widened(jump_ref[l], jl_ref, jr_ref, l)
        o_ref[1, l] = pltpu.roll(value, window - SECTIONS // 2, 0) if narrow else value
    sends.append(send(12, o_ref.at[1, :, filled], x_ref.at[1, :, filled], later, space))

    def arrived(l):
        value = x_ref[1, l]
        if narrow:
            value = jnp.concatenate([value[:full], jnp.zeros((window - full, lanes), value.dtype)], 0)
            value = pltpu.roll(value, SECTIONS // 2, 0)
        return value

    sends[15].wait_recv()
    results = coarse_step(arrived, own=False)
    for l in range(levels):
        coarse_ref[1, l] = results[l] + coarse_ref[0, l]
    results = coarse_step(lambda l: coarse_ref[1, l])

    chunk = levels // SECTIONS
    shape = (nf, window)
    spread_rows = exact(iota(shape, 0) // COARSEN + SECTIONS == iota(shape, 1), 1.0)
    shape = (lanes, lat)
    group = iota(shape, 1) // COARSEN
    spread0 = exact(group == iota(shape, 0), 1.0)
    spread1 = exact(group + lc == iota(shape, 0), 1.0)
    for c in range(SECTIONS):
        stacked = []
        for l in range(c * chunk, (c + 1) * chunk):
            stacked.append([
                dot(spread_rows, part).astype(jnp.bfloat16) for part in split(results[l] - first_ref[l])
            ])
        parts = [jnp.concatenate(same, 0) for same in zip(*stacked)]
        for t, spread in enumerate((spread0, spread1)):
            value = sum(dot(part, spread) for part in parts).reshape(chunk, nf, lat)
            part = pl.ds(c * chunk, chunk)
            out_ref[0, t, part] = out_ref[0, t, part] + value
    for copy in sends:
        copy.wait_send()
    for index in range(pieces):
        piece(index).wait_send()


def shards(start_states, wet_levels, advection, forcing, rates):
    _, tracers, levels, nf, lat = start_states.shape
    nc = nf // COARSEN
    lanes = 2 * (lat // COARSEN)
    window = -(-(nc + 2 * SECTIONS) // 8) * 8
    rows = nf + EDGE
    f32 = jnp.float32
    packed = pltpu.VMEM((levels, EDGE, lat), f32)
    coarse = pltpu.VMEM((levels, window, lanes), f32)
    edge = pltpu.VMEM((levels // 2, 8, lanes), f32)
    shifts = pltpu.VMEM((2, levels, window, lanes), f32)
    copies = 16 + levels // CHUNK
    vmem = pl.BlockSpec(memory_space=pltpu.VMEM)
    hbm = pl.BlockSpec(memory_space=pltpu.HBM)
    return pl.pallas_call(
        kernel,
        out_shape=jax.ShapeDtypeStruct(start_states.shape, f32),
        in_specs=[hbm] * 5,
        out_specs=vmem,
        scratch_shapes=[
            pltpu.VMEM((tracers, levels, rows, lat), f32),
            pltpu.VMEM((STEPS, tracers, levels + 2, rows, lat), f32),
            pltpu.VMEM((3, rows, lat), f32),
            pltpu.VMEM((levels, rows, lat), f32),
            pltpu.VMEM((3, nf + 2 * WIDE, lat), f32),
            pltpu.VMEM((2, tracers, levels, EDGE, lat), f32),
            pltpu.VMEM((2, levels, EDGE, lat), f32),
            packed, packed,
            pltpu.VMEM((11, levels, window, lanes), f32),
            coarse, coarse, shifts, edge, edge, edge, edge,
            coarse, edge, edge, shifts, shifts, edge, edge, edge, edge,
            pltpu.VMEM((nf, lat), jnp.int32),
            pltpu.SMEM(rates.shape, f32),
            pltpu.SemaphoreType.DMA((6,)),
            pltpu.SemaphoreType.DMA((copies,)),
            pltpu.SemaphoreType.DMA((copies,)),
        ],
        compiler_params=pltpu.CompilerParams(
            collective_id=0, has_side_effects=True, vmem_limit_bytes=64 * 1024 * 1024
        ),
    )(start_states, wet_levels, advection, forcing, rates)

def solution(mesh):
    return jax.shard_map(
        shards,
        mesh=mesh,
        in_specs=(
            P("tm", None, None, "space", None),
            P("space", None),
            P("space", None),
            P("space", None),
            P(),
        ),
        out_specs=P("tm", None, None, "space", None),
        check_vma=False,
    )
```

```python
import math

import jax
import jax.numpy as jnp
from jax import lax
from jax.experimental import pallas as pl
from jax.experimental.pallas import tpu as pltpu
from jax.sharding import PartitionSpec as P

STEPS = 4
SECTIONS = 4
COARSEN = 4
RELAX = 0.2
EDGE = 8
LANES = 128
CHUNK = 2
WIDE = COARSEN * SECTIONS
MESH = pl.DeviceIdType.MESH


def season_at(position, year):
    return 1.0 + 0.6 * jnp.sin(2.0 * math.pi * position / year)


def iota(shape, dim):
    return lax.broadcasted_iota(jnp.int32, shape, dim)


def dot(a, b):
    return jnp.dot(a, b, preferred_element_type=jnp.float32)


def split(value):
    parts = []
    for _ in range(3):
        part = value.astype(jnp.bfloat16)
        value = value - part.astype(jnp.float32)
        parts.append(part)
    return parts


def exact(flags, value):
    return jnp.where(flags, value, 0.0).astype(jnp.bfloat16)


def fold_rows(weights, value):
    if weights.shape[1] > value.shape[0]:
        rest = weights.shape[1] - value.shape[0]
        value = jnp.concatenate([value, jnp.zeros((rest, value.shape[1]), value.dtype)], 0)
    return dot(jnp.concatenate([weights] * 3, 1), jnp.concatenate(split(value), 0))


def kernel(
    start_ref, wet_hbm, flow_hbm, forcing_hbm, rates_hbm, out_hbm, out_ref,
    s_ref, state_ref, ring_ref, diag_ref, aux_ref, edge_ref, pack_ref, hr_ref, hl_ref,
    coef_ref, first_ref, jump_ref, x_ref, xl_ref, xr_ref, jl_ref, jr_ref,
    jn_ref, jnl_ref, jnr_ref, coarse_ref, o_ref, ol_ref, or_ref, pl_ref, pr_ref,
    wet_ref, rates_ref, local_sem, send_sem, recv_sem,
):
    _, tracers, levels, nf, lat = out_ref.shape
    nc = nf // COARSEN
    lc = lat // COARSEN
    lanes = 2 * lc
    window = coef_ref.shape[2]
    rows = nf + EDGE
    tm, n_tm = lax.axis_index("tm"), lax.axis_size("tm")
    space, n_space = lax.axis_index("space"), lax.axis_size("space")
    after, before = lax.rem(tm + 1, n_tm), lax.rem(tm + n_tm - 1, n_tm)
    later, earlier = lax.rem(tm + 2, n_tm), lax.rem(tm + n_tm - 2, n_tm)
    right, left = lax.rem(space + 1, n_space), lax.rem(space + n_space - 1, n_space)

    barrier = pltpu.get_barrier_semaphore()
    sources = [(tm, left), (tm, right)]
    sources += [(i, j) for i in (before, earlier) for j in (space, left, right)]
    for i, j in sources:
        pl.semaphore_signal(barrier, inc=1, device_id=(i, j), device_id_type=MESH)

    mid = pl.ds(WIDE, nf)
    loads = [
        pltpu.make_async_copy(src, dst, local_sem.at[i])
        for i, (src, dst) in enumerate((
            (wet_hbm, wet_ref),
            (flow_hbm, aux_ref.at[1, mid, :]),
            (forcing_hbm, aux_ref.at[2, mid, :]),
            (rates_hbm, rates_ref),
            (start_ref.at[0, :, :, pl.ds(0, EDGE), :], edge_ref.at[0]),
            (start_ref.at[0, :, :, pl.ds(nf - EDGE, EDGE), :], edge_ref.at[1]),
        ))
    ]
    for load in loads:
        load.start()
    where = jnp.minimum(iota((8, 128), 1).astype(jnp.float32) + 0.5, STEPS + 0.5)
    where = jnp.where(where > STEPS, STEPS * 0.5, where)
    begin = (before * STEPS).astype(jnp.float32)
    season_ref = season_at(begin + where, STEPS * n_tm)
    begin = (earlier * STEPS).astype(jnp.float32)
    season_before = season_at(begin + where, STEPS * n_tm)
    zero = jnp.zeros((tracers, rows, lat), jnp.float32)
    for step in range(STEPS):
        state_ref[step, :, 0] = zero
        state_ref[step, :, levels + 1] = zero
    for load in loads[:3]:
        load.wait()
    aux_ref[0, mid, :] = wet_ref[...].astype(jnp.float32)
    loads[4].wait()
    loads[5].wait()
    upper_half = iota((EDGE, lat), 0) < COARSEN
    for l in range(levels):
        pack_ref[0, l] = jnp.where(
            upper_half, edge_ref[0, 0, l], pltpu.roll(edge_ref[0, 1, l], COARSEN, 0)
        )
        pack_ref[1, l] = jnp.where(
            upper_half, pltpu.roll(edge_ref[1, 0, l], COARSEN, 0), edge_ref[1, 1, l]
        )
    pl.semaphore_wait(barrier, len(sources))

    def send(index, src, dst, i, j):
        copy = pltpu.make_async_remote_copy(
            src_ref=src, dst_ref=dst, send_sem=send_sem.at[index], recv_sem=recv_sem.at[index],
            device_id=(i, j), device_id_type=MESH,
        )
        copy.start()
        return copy

    sends = [
        send(0, aux_ref.at[:, pl.ds(nf, WIDE), :], aux_ref.at[:, pl.ds(0, WIDE), :], tm, right),
        send(1, aux_ref.at[:, pl.ds(WIDE, WIDE), :],
             aux_ref.at[:, pl.ds(WIDE + nf, WIDE), :], tm, left),
        send(2, pack_ref.at[0], hr_ref, after, left),
        send(3, pack_ref.at[1], hl_ref, after, right),
    ]

    def piece(index):
        part = pl.ds(index * CHUNK, CHUNK)
        return pltpu.make_async_remote_copy(
            src_ref=start_ref.at[0, :, part], dst_ref=s_ref.at[:, part, pl.ds(0, nf), :],
            send_sem=send_sem.at[16 + index], recv_sem=recv_sem.at[16 + index],
            device_id=(after, space), device_id_type=MESH,
        )

    pieces = levels // CHUNK
    for index in range(pieces):
        piece(index).start()

    loads[3].wait()
    sends[0].wait_recv()
    sends[1].wait_recv()
    half = iota((EDGE, lat), 0) < COARSEN
    for i in range(3):
        ring_ref[i, pl.ds(0, nf), :] = aux_ref[i, mid, :]
        ring_ref[i, pl.ds(nf, EDGE), :] = jnp.where(
            half, aux_ref[i, pl.ds(WIDE + nf, EDGE), :], aux_ref[i, pl.ds(WIDE - EDGE, EDGE), :]
        )
    wide = ring_ref[0]
    lane = iota((rows, lat), 1)
    wet_e = pltpu.roll(wide, rows - 1, 0)
    wet_w = pltpu.roll(wide, 1, 0)
    wet_n = jnp.where(lane == lat - 1, 0.0, pltpu.roll(wide, lat - 1, 1))
    wet_s = jnp.where(lane == 0, 0.0, pltpu.roll(wide, 1, 1))
    flow = ring_ref[1]
    for l in range(levels):
        k = rates_ref[0, l]
        west = jnp.where(wet_w > l, 1.0, 0.0)
        count = west
        for other in (wet_e, wet_n, wet_s):
            count = count + jnp.where(other > l, 1.0, 0.0)
        total = 1.0 - k * count - flow * west
        if l:
            total = total - rates_ref[1, l - 1]
        if l < levels - 1:
            total = total - jnp.where(wide > l + 1, rates_ref[1, l], 0.0)
        diag_ref[l] = total
    quarter = 1.0 / COARSEN
    group, folded = iota((lat, lanes), 0) // COARSEN, iota((lat, lanes), 1)
    fold0 = exact(group == folded, quarter)
    fold1 = exact(group + lc == folded, quarter)
    both = fold0 + fold1

    def gather_rows(count, base):
        shape = (window, count)
        return exact(iota(shape, 1) // COARSEN + base == iota(shape, 0), quarter)

    def fold_lat(nutrient, organic):
        pairs = zip(split(nutrient), split(organic))
        return sum(dot(first, fold0) + dot(second, fold1) for first, second in pairs)

    row = iota((window, lanes), 0)
    col = iota((window, lanes), 1)
    inner = (row >= SECTIONS) & (row < SECTIONS + nc)
    to_right = iota((8, lanes), 0) < SECTIONS
    tail = iota((8, lanes), 0) + (window - 8)
    to_left = (tail >= SECTIONS + nc) & (tail < 2 * SECTIONS + nc)

    wide_rows = gather_rows(nf + 2 * WIDE, 0)
    c_flow = fold_rows(wide_rows, fold_lat(aux_ref[1], aux_ref[1])) * (STEPS / COARSEN)
    c_forcing = fold_rows(wide_rows, fold_lat(aux_ref[2], aux_ref[2]))
    wet = aux_ref[0]
    masks = [
        dot(wide_rows, dot(exact(wet > l, 1.0), both).astype(jnp.bfloat16)) for l in range(levels)
    ]
    season = season_ref[0, STEPS]
    is_nutrient = col < lc
    edge_n = (col == lc - 1) | (col == lanes - 1)
    edge_s = (col == 0) | (col == lc)
    for l in range(levels):
        m = masks[l]
        k = rates_ref[0, l] * (STEPS / COARSEN**2)
        g = rates_ref[2, l] * STEPS * season
        g_before = rates_ref[2, l] * STEPS * season_before[0, STEPS]
        r = rates_ref[3, l] * STEPS
        q = RELAX * STEPS if l == 0 else 0.0
        m_w = pltpu.roll(m, 1, 0)
        east = k * pltpu.roll(m, window - 1, 0)
        west = (k + c_flow) * m_w
        north = k * jnp.where(edge_n, 0.0, pltpu.roll(m, lanes - 1, 1))
        south = k * jnp.where(edge_s, 0.0, pltpu.roll(m, 1, 1))
        total = 1.0 - east - west - north - south
        if l < levels - 1:
            down = rates_ref[1, l] * STEPS * masks[l + 1]
            total = total - down
            coef_ref[4, l] = down
        if l:
            up = rates_ref[1, l - 1] * STEPS * masks[l - 1]
            total = total - up
            coef_ref[5, l] = up
        coef_ref[0, l] = east
        coef_ref[1, l] = west
        coef_ref[2, l] = north
        coef_ref[3, l] = south
        coef_ref[6, l] = total
        coef_ref[7, l] = m * jnp.where(is_nutrient, 1.0 - g - q, 1.0 - r)
        coef_ref[8, l] = m * jnp.where(is_nutrient, r, g)
        coef_ref[9, l] = m * jnp.where(is_nutrient, 1.0 - g_before - q, 1.0 - r)
        coef_ref[10, l] = m * jnp.where(is_nutrient, r, g_before)
    surface = masks[0] * jnp.where(is_nutrient, RELAX * STEPS * c_forcing, 0.0)

    sends[2].wait_recv()
    sends[3].wait_recv()
    padded_rows = -(-rows // 16) * 16
    at, ring = iota((window, padded_rows), 0), iota((window, padded_rows), 1)
    start_rows = exact(
        ((ring < nf + COARSEN) & (ring // COARSEN + SECTIONS == at))
        | ((ring >= nf + COARSEN) & (ring < rows) & (at == SECTIONS - 1)),
        quarter,
    )

    centre_rows = gather_rows(nf, SECTIONS)

    def halo_parts(value):
        low = jnp.where(to_right, pltpu.roll(value, window - nc, 0)[:8], 0.0)
        high = jnp.where(to_left, pltpu.roll(value, nc, 0)[window - 8:], 0.0)
        return low, high

    full = -(-(nc + SECTIONS) // 8) * 8

    def put_halos(values, low_ref, high_ref, first=0):
        parts = [halo_parts(value) for value in values]
        for l in range(len(parts) // 2):
            for ref, one, two in zip((low_ref, high_ref), parts[2 * l], parts[2 * l + 1]):
                ref[first + l] = one + pltpu.roll(two, SECTIONS, 0)

    def get_halo(ref, flags, l):
        value = ref[l // 2]
        if l % 2:
            value = pltpu.roll(value, SECTIONS, 0)
        return jnp.where(flags, value, 0.0)

    def widened(value, low_ref, high_ref, l):
        low, high = get_halo(low_ref, to_right, l), get_halo(high_ref, to_left, l)
        pieces = [value[:8] + low, value[8:window - 8]]
        pieces.append(value[window - 8:] + high if full == window else high)
        return jnp.concatenate(pieces, 0)

    def fold_end(first, count):
        part = pl.ds(first, count)
        flat = (count * nf, lat)
        folds = fold_lat(out_ref[0, 0, part].reshape(flat), out_ref[0, 1, part].reshape(flat))
        for j in range(count):
            o_ref[0, first + j] = fold_rows(centre_rows, folds[j * nf:(j + 1) * nf])

    def fold_start(index):
        part = pl.ds(index * CHUNK, CHUNK)
        flat = (CHUNK * rows, lat)
        folds = fold_lat(s_ref[0, part].reshape(flat), s_ref[1, part].reshape(flat))
        for j in range(CHUNK):
            value = fold_rows(start_rows, folds[j * rows:(j + 1) * rows])
            first_ref[index * CHUNK + j] = value

    def arrive(index):
        piece(index).wait_recv()
        for j in range(CHUNK):
            l = index * CHUNK + j
            high, low = hr_ref[l], hl_ref[l]
            s_ref[0, l, pl.ds(nf, EDGE), :] = jnp.where(half, high, pltpu.roll(low, COARSEN, 0))
            s_ref[1, l, pl.ds(nf, EDGE), :] = jnp.where(half, pltpu.roll(high, COARSEN, 0), low)
            here = ring_ref[0] > jnp.asarray(l, jnp.float32)
            for t in range(tracers):
                state_ref[0, t, l + 1] = jnp.where(here, s_ref[t, l], 0.0)

    sub = iota((EDGE, LANES), 0)
    lane = iota((EDGE, LANES), 1)
    blocks = rows // EDGE
    tiles = lat // LANES

    def fine_level(step, l):
        season = season_ref[0, step]
        k, v, g, r = (rates_ref[i, l] for i in range(4))
        upper = rates_ref[1, lax.rem(l + levels - 1, levels)]
        lf = l.astype(jnp.float32)
        grown = g * season
        q = jnp.where(l == 0, RELAX, 0.0)
        kept, stays = 1.0 - grown - q, 1.0 - r
        for x in range(tiles):
            across = pl.ds(x * LANES, LANES)
            cells, norths, souths = [], [], []
            for t in range(tracers):
                cell = [
                    state_ref[step, t, l + 1, pl.ds(b * EDGE, EDGE), across] for b in range(blocks)
                ]
                cells.append(
                    (cell, [pltpu.roll(c, EDGE - 1, 0) for c in cell],
                     [pltpu.roll(c, 1, 0) for c in cell])
                )
            for b in range(blocks if step < STEPS - 1 else blocks - 1):
                down_rows = pl.ds(b * EDGE, EDGE)
                centre = diag_ref[l, down_rows, across]
                speed = ring_ref[1, down_rows, across] + k
                here = ring_ref[0, down_rows, across] > lf
                mixed = []
                for t in range(tracers):
                    cell, fore, back = cells[t]
                    u = cell[b]
                    east = jnp.where(sub == EDGE - 1, fore[(b + 1) % blocks], fore[b])
                    west = jnp.where(sub == 0, back[(b + blocks - 1) % blocks], back[b])
                    if x + 1 < tiles:
                        ahead = state_ref[step, t, l + 1, down_rows, pl.ds((x + 1) * LANES, LANES)]
                        ahead = pltpu.roll(ahead, LANES - 1, 1)
                    else:
                        ahead = 0.0
                    if x:
                        behind = state_ref[step, t, l + 1, down_rows, pl.ds((x - 1) * LANES, LANES)]
                        behind = pltpu.roll(behind, 1, 1)
                    else:
                        behind = 0.0
                    north = jnp.where(lane == LANES - 1, ahead, pltpu.roll(u, LANES - 1, 1))
                    south = jnp.where(lane == 0, behind, pltpu.roll(u, 1, 1))
                    mixed.append(
                        centre * u + k * (east + north + south) + speed * west
                        + v * state_ref[step, t, l + 2, down_rows, across]
                        + upper * state_ref[step, t, l, down_rows, across]
                    )
                nutrient = mixed[0] * kept + r * mixed[1] + q * ring_ref[2, down_rows, across]
                organic = mixed[1] * stays + grown * mixed[0]
                nutrient = jnp.where(here, nutrient, 0.0)
                organic = jnp.where(here, organic, 0.0)
                if step < STEPS - 1:
                    state_ref[step + 1, 0, l + 1, down_rows, across] = nutrient
                    state_ref[step + 1, 1, l + 1, down_rows, across] = organic
                else:
                    out_ref[0, 0, l, down_rows, across] = nutrient
                    out_ref[0, 1, l, down_rows, across] = organic

    lag = 1 - (-STEPS // CHUNK)
    early = (pieces - lag) * CHUNK
    filled = pl.ds(0, full)

    def ends(first, count, index):
        part, pairs = pl.ds(first, count), pl.ds(first // 2, count // 2)
        routes = (
            (o_ref.at[0, part, filled], x_ref.at[0, part, filled], space),
            (ol_ref.at[pairs], xl_ref.at[pairs], right),
            (or_ref.at[pairs], xr_ref.at[pairs], left),
        )
        return [
            pltpu.make_async_remote_copy(
                src_ref=src, dst_ref=dst, send_sem=send_sem.at[index + i],
                recv_sem=recv_sem.at[index + i], device_id=(later, j), device_id_type=MESH,
            )
            for i, (src, dst, j) in enumerate(routes)
        ]

    arrive(0)

    def diagonal(d, carry):
        @pl.when((lax.rem(d + 1, CHUNK) == 0) & (d + 1 < levels))
        def _():
            index = (d + 1) // CHUNK
            fold_start(index - 1)

            @pl.when(index >= lag)
            def _():
                fold_end((index - lag) * CHUNK, CHUNK)

            arrive(index)

            @pl.when(index == pieces - 1)
            def _():
                put_halos([o_ref[0, l] for l in range(early)], ol_ref, or_ref)
                for copy in ends(0, early, 13):
                    copy.start()

        for step in range(STEPS):
            @pl.when((d >= step) & (d < levels + step))
            def _():
                fine_level(step, d - step)

        return carry

    lax.fori_loop(0, levels + STEPS - 1, diagonal, 0)

    fold_end((pieces - lag) * CHUNK, lag * CHUNK)
    put_halos([o_ref[0, l] for l in range(early, levels)], ol_ref, or_ref, early // 2)
    sends += [copy for copy in ends(0, early, 13)]
    for copy in ends(early, levels - early, 4):
        copy.start()
        sends.append(copy)

    def coarse_step(load_level, own=True):
        fields = [load_level(l) for l in range(levels)]
        results = []
        for l in range(levels):
            u = fields[l]
            w = coef_ref[6, l] * u
            w = w + coef_ref[0, l] * pltpu.roll(u, window - 1, 0)
            w = w + coef_ref[1, l] * pltpu.roll(u, 1, 0)
            w = w + coef_ref[2, l] * pltpu.roll(u, lanes - 1, 1)
            w = w + coef_ref[3, l] * pltpu.roll(u, 1, 1)
            if l < levels - 1:
                w = w + coef_ref[4, l] * fields[l + 1]
            if l:
                w = w + coef_ref[5, l] * fields[l - 1]
            kept, mixed = (7, 8) if own else (9, 10)
            value = coef_ref[kept, l] * w + coef_ref[mixed, l] * pltpu.roll(w, lc, 1)
            if l == 0:
                value = value + surface
            results.append(value)
        return results

    fold_start(pieces - 1)
    jumps = []
    for l, value in enumerate(coarse_step(lambda l: first_ref[l])):
        value = jnp.where(inner, value, 0.0)
        first_ref[l] = value
        jump = o_ref[0, l] - value
        jump_ref[l] = jump
        jumps.append(jump)
    put_halos(jumps, pl_ref, pr_ref)
    sends += [
        send(9, jump_ref.at[:, filled], jn_ref.at[:, filled], after, space),
        send(10, pl_ref, jnl_ref, after, right),
        send(11, pr_ref, jnr_ref, after, left),
        send(7, pl_ref, jl_ref, tm, right),
        send(8, pr_ref, jr_ref, tm, left),
    ]

    for copy in sends[4:10]:
        copy.wait_recv()
    results = coarse_step(lambda l: widened(x_ref[0, l], xl_ref, xr_ref, l), own=False)
    for copy in sends[10:13]:
        copy.wait_recv()
    for l in range(levels):
        jump = widened(jn_ref[l], jnl_ref, jnr_ref, l)
        coarse_ref[0, l] = jump
        coarse_ref[1, l] = results[l] + jump
    results = coarse_step(lambda l: coarse_ref[1, l])
    for copy in sends[13:15]:
        copy.wait_recv()
    narrow = full < window
    for l in range(levels):
        value = results[l] + widened(jump_ref[l], jl_ref, jr_ref, l)
        o_ref[1, l] = pltpu.roll(value, window - SECTIONS // 2, 0) if narrow else value
    sends.append(send(12, o_ref.at[1, :, filled], x_ref.at[1, :, filled], later, space))

    def arrived(l):
        value = x_ref[1, l]
        if narrow:
            value = jnp.concatenate([value[:full], jnp.zeros((window - full, lanes), value.dtype)], 0)
            value = pltpu.roll(value, SECTIONS // 2, 0)
        return value

    sends[15].wait_recv()
    results = coarse_step(arrived, own=False)
    for l in range(levels):
        coarse_ref[1, l] = results[l] + coarse_ref[0, l]
    results = coarse_step(lambda l: coarse_ref[1, l])

    chunk = levels // SECTIONS
    shape = (nf, window)
    spread_rows = exact(iota(shape, 0) // COARSEN + SECTIONS == iota(shape, 1), 1.0)
    shape = (lanes, lat)
    group = iota(shape, 1) // COARSEN
    spread0 = exact(group == iota(shape, 0), 1.0)
    spread1 = exact(group + lc == iota(shape, 0), 1.0)
    stores = []
    for c in range(SECTIONS):
        stacked = []
        for l in range(c * chunk, (c + 1) * chunk):
            stacked.append([
                dot(spread_rows, part).astype(jnp.bfloat16) for part in split(results[l] - first_ref[l])
            ])
        parts = [jnp.concatenate(same, 0) for same in zip(*stacked)]
        for t, spread in enumerate((spread0, spread1)):
            value = sum(dot(part, spread) for part in parts).reshape(chunk, nf, lat)
            part = pl.ds(c * chunk, chunk)
            out_ref[0, t, part] = out_ref[0, t, part] + value
        part = pl.ds(c * chunk, chunk)
        store = pltpu.make_async_copy(
            out_ref.at[:, :, part], out_hbm.at[:, :, part], local_sem.at[6 + c]
        )
        store.start()
        stores.append(store)
    for store in stores:
        store.wait()
    for copy in sends:
        copy.wait_send()
    for index in range(pieces):
        piece(index).wait_send()


def shards(start_states, wet_levels, advection, forcing, rates):
    _, tracers, levels, nf, lat = start_states.shape
    nc = nf // COARSEN
    lanes = 2 * (lat // COARSEN)
    window = -(-(nc + 2 * SECTIONS) // 8) * 8
    rows = nf + EDGE
    f32 = jnp.float32
    packed = pltpu.VMEM((levels, EDGE, lat), f32)
    coarse = pltpu.VMEM((levels, window, lanes), f32)
    edge = pltpu.VMEM((levels // 2, 8, lanes), f32)
    shifts = pltpu.VMEM((2, levels, window, lanes), f32)
    copies = 16 + levels // CHUNK
    hbm = pl.BlockSpec(memory_space=pltpu.HBM)
    return pl.pallas_call(
        kernel,
        out_shape=jax.ShapeDtypeStruct(start_states.shape, f32),
        in_specs=[hbm] * 5,
        out_specs=hbm,
        scratch_shapes=[
            pltpu.VMEM((1, tracers, levels, nf, lat), f32),
            pltpu.VMEM((tracers, levels, rows, lat), f32),
            pltpu.VMEM((STEPS, tracers, levels + 2, rows, lat), f32),
            pltpu.VMEM((3, rows, lat), f32),
            pltpu.VMEM((levels, rows, lat), f32),
            pltpu.VMEM((3, nf + 2 * WIDE, lat), f32),
            pltpu.VMEM((2, tracers, levels, EDGE, lat), f32),
            pltpu.VMEM((2, levels, EDGE, lat), f32),
            packed, packed,
            pltpu.VMEM((11, levels, window, lanes), f32),
            coarse, coarse, shifts, edge, edge, edge, edge,
            coarse, edge, edge, shifts, shifts, edge, edge, edge, edge,
            pltpu.VMEM((nf, lat), jnp.int32),
            pltpu.SMEM(rates.shape, f32),
            pltpu.SemaphoreType.DMA((6 + SECTIONS,)),
            pltpu.SemaphoreType.DMA((copies,)),
            pltpu.SemaphoreType.DMA((copies,)),
        ],
        compiler_params=pltpu.CompilerParams(
            collective_id=0, has_side_effects=True, vmem_limit_bytes=64 * 1024 * 1024
        ),
    )(start_states, wet_levels, advection, forcing, rates)

def solution(mesh):
    return jax.shard_map(
        shards,
        mesh=mesh,
        in_specs=(
            P("tm", None, None, "space", None),
            P("space", None),
            P("space", None),
            P("space", None),
            P(),
        ),
        out_specs=P("tm", None, None, "space", None),
        check_vma=False,
    )
```
